512 devices in a mesh: row: 32 (over z, y_hi), col: 16 (over x, y_lo, core).
Axes of the slice: x: 4, y: 4 (y_hi: 2, y_lo: 2; y = y_hi * 2 + y_lo), z: 16, core: 2. Of those that a mesh axis runs over, the one named last changes fastest.
Arguments:
- factor_band: float32 [4096, 131072], P('row', 'col'), may hold values from -0.015625 to 0.015625
- normals: float32 [131072, 384], P('col', 'row'), may hold values from -6 to 6
- site_mean: float32 [4096], P('row'), may hold values from 5 to 10
- site_spread: float32 [4096], P('row'), may hold values from 1 to 4
- site_capacity: float32 [4096], P('row'), may hold values from 0.1 to 1
- site_kind: int32 [4096], P('row'), may hold values 0 or 1
- site_plant: int32 [4096], P('row'), may hold values from 0 to 2047
Outputs:
- plant_output: float32 [384, 2048], P('col', 'row')
The draws below stay inside these ranges and needn't reach their ends.
All inputs are finite; a program needn't handle non-finite values. No bound on the sum of `site_kind` on one device may be relied on, other than what follows from the above.
Results may differ from the reference program's by a relative error of at most 0.000096.
Values sent between devices are 32-bit elements; how exact they have to be, the bound alone decides.
A program may use at most 128 MiB of HBM per device.

```python
import math
import jax
import jax.numpy as jnp
import numpy as np
from jax import lax

N = 131072
PLANTS = 2048
BAND = 4096
SAMPLES = 384


def plant(drawn, key, low, high):
    index_at = [jax.random.randint(jax.random.fold_in(key, axis), (), 0, length) for axis, length in enumerate(drawn.shape)]
    main_axis = drawn.shape.index(max(drawn.shape))
    neighbour = index_at[:main_axis] + [(index_at[main_axis] + 1) % drawn.shape[main_axis]] + index_at[main_axis + 1:]
    return drawn.at[tuple(index_at)].set(low).at[tuple(neighbour)].set(high)


def block_levels(rng, dims, pieces, low, largest):
    def one(dim, blocks):
        steps = jax.random.uniform(jax.random.fold_in(jax.random.fold_in(rng, 6), dim), (blocks,), jnp.float32, low / len(pieces), largest / len(pieces))
        return jnp.repeat(jnp.exp(steps), dims[dim] // blocks).reshape((-1,) + (1,) * (len(dims) - dim - 1))

    loudness = one(*pieces[0])
    for cut in pieces[1:]:
        loudness = loudness * one(*cut)
    return loudness


def rank_bounds(number_of, skew):
    portions = [(1 << 20) // math.isqrt(standing ** skew) + 1 for standing in range(1, number_of + 1)]
    scale = 1 + sum(portions) // (1 << 30)
    return np.cumsum(np.array([max(1, weight // scale) for weight in portions]))


def ranked(own_key, dims, count, slope):
    listing = rank_bounds(count, slope)
    pick = jax.random.randint(jax.random.fold_in(own_key, 1), dims, 0, int(listing[count - 1]))
    grade = jnp.searchsorted(jnp.asarray(listing, jnp.int32), pick, side="right")
    return jax.random.permutation(jax.random.fold_in(own_key, 2), count)[grade].astype(jnp.int32)


def bell_draw(key, shape, width, most, pieces=(), kind=jnp.bfloat16):
    result = width * jax.random.normal(key, shape, jnp.float32)
    if pieces:
        result = result * block_levels(key, shape, pieces, -0.22, 0.18)
    return jnp.clip(result, -most, most).astype(kind)


def setup_inputs(seed: int = 0) -> dict:
    arg_keys = jax.random.split(jax.random.key(seed), 8)
    return {
        "factor_band": bell_draw(arg_keys[0], (BAND, N), N ** -0.5, 0.015625, ((0, 32), (1, 16)), jnp.float32),
        "normals": bell_draw(arg_keys[1], (N, SAMPLES), 1.0, 6.0, ((0, 16), (1, 32)), jnp.float32),
        "site_mean": jnp.clip(jnp.exp(math.log(10.0) - 0.6931472 * jax.random.uniform(arg_keys[2], (BAND,), jnp.float32) ** block_levels(arg_keys[2], (BAND,), ((0, 32),), -0.2, 0.2)), 5.0, 10.0),
        "site_spread": jnp.clip(jnp.exp(math.log(4.0) - 1.3862944 * jax.random.uniform(arg_keys[3], (BAND,), jnp.float32) ** block_levels(arg_keys[3], (BAND,), ((0, 32),), -0.2, 0.2)), 1.0, 4.0),
        "site_capacity": jnp.clip(jnp.exp(math.log(1.0) - 2.3025851 * jax.random.uniform(arg_keys[4], (BAND,), jnp.float32) ** block_levels(arg_keys[4], (BAND,), ((0, 32),), -0.2, 0.2)), 0.1, 1.0),
        "site_kind": plant((jax.random.randint(arg_keys[5], (BAND,), 0, 3) < 1).astype(jnp.int32), jax.random.fold_in(arg_keys[5], 1), 0, 1),
        "site_plant": plant(ranked(arg_keys[6], (BAND,), PLANTS, 1), jax.random.fold_in(arg_keys[6], 3), 0, PLANTS - 1).astype(jnp.int32),
    }


def reference(factor_band, normals, site_mean, site_spread, site_capacity, site_kind, site_plant):
    samples = lax.dot_general(normals, factor_band, (((0,), (1,)), ((), ())), precision=lax.Precision.HIGHEST, preferred_element_type=jnp.float32)
    speed = site_mean[None, :] + site_spread[None, :] * samples
    positive = jnp.maximum(speed, 0.0)
    wind = jnp.clip((positive * positive * positive - 27.0) / (1728.0 - 27.0), 0.0, 1.0)
    solar = jnp.clip(speed / 12.0, 0.0, 1.0)
    power = jnp.where(site_kind[None, :] == 1, solar, wind) * site_capacity[None, :]
    totals = jax.ops.segment_sum(power.T, site_plant, num_segments=PLANTS)
    return totals.T
```

```python
import functools

import jax
import jax.numpy as jnp
from jax import lax
from jax.experimental import pallas as pl
from jax.experimental.pallas import tpu as pltpu
from jax.sharding import PartitionSpec as P

MESH = pl.DeviceIdType.MESH
LAG = 1


def split_bf16(v):
    hi = v.astype(jnp.bfloat16)
    return hi, (v - hi.astype(jnp.float32)).astype(jnp.bfloat16)


def nt_dot(a, b):
    return lax.dot_general(a, b, (((1,), (1,)), ((), ())), preferred_element_type=jnp.float32)


def kernel(
    nz, nc, kh, plants,
    f_ref, n_ref, mean_ref, spread_ref, cap_ref, kind_ref, plant_ref, out_ref,
    nown, nbuf, bsend, brecv, fown, frecv, fh, fl, par, onehot, acc, rsend, rrecv, zsend, zrecv,
    loc_sem, nx_send, nx_recv, fx_send, fx_recv, ring_send, ring_recv, r_send, r_recv, z_send, z_recv,
):
    half = nz // 2
    zero = half - 1
    near = half - 2
    peers = 2 * nc
    rows = 2 * nz
    row, col = lax.axis_index("row"), lax.axis_index("col")
    z, yh = row // 2, lax.rem(row, 2)
    partner = row + 1 - 2 * yh
    right = lax.rem(z + 1, nz) * 2 + yh
    left = lax.rem(z + nz - 1, nz) * 2 + yh
    mine = pl.multiple_of(yh * kh, kh)
    other = pl.multiple_of((1 - yh) * kh, kh)
    ua, up = 2 * yh, 2 - 2 * yh

    load_a = pltpu.make_async_copy(n_ref.at[pl.ds(0, 8), pl.ds(mine, kh)], nbuf.at[zero, ua], loc_sem.at[0])
    load_n = pltpu.make_async_copy(n_ref, nown, loc_sem.at[1])
    load_f = pltpu.make_async_copy(f_ref.at[:, pl.ds(mine, kh)], fown, loc_sem.at[2])
    load_a.start()
    load_n.start()
    load_f.start()

    barrier = pltpu.get_barrier_semaphore()

    @pl.loop(0, peers)
    def _(i):
        r, c = z * 2 + i // nc, lax.rem(i, nc)

        @pl.when(jnp.logical_or(r != row, c != col))
        def _():
            pl.semaphore_signal(barrier, inc=1, device_id=(r, c), device_id_type=MESH)

    @pl.loop(0, rows)
    def _(r):
        @pl.when(r != row)
        def _():
            pl.semaphore_signal(barrier, inc=1, device_id=(r, col), device_id_type=MESH)

    row_of = lax.broadcasted_iota(jnp.int32, (8, 128), 0)
    packed = jnp.zeros((8, 128), jnp.float32)
    for i, ref in enumerate((mean_ref, spread_ref, cap_ref, kind_ref, plant_ref)):
        packed = jnp.where(row_of == i, ref[...].astype(jnp.float32).reshape(1, 128), packed)
    par[yh] = packed
    load_n.wait()
    q = kh // 2
    bsend[0:4, :] = nown[8:12, pl.ds(other, q)]
    bsend[4:8, :] = nown[8:12, pl.ds(pl.multiple_of(other + q, q), q)]
    load_a.wait()

    pl.semaphore_wait(barrier, peers - 1 + rows - 1)

    def to_partner(src, dst, i):
        return pltpu.make_async_remote_copy(
            src, dst, nx_send.at[i], nx_recv.at[i], device_id=(partner, col), device_id_type=MESH
        )

    def ring(s, h, way):
        unit = (ua, up, 1)[s]
        slot = zero - h if way == 0 else zero + h
        to = slot - 1 if way == 0 else slot + 1
        if h < half - 1:
            src, dst = nbuf.at[slot, unit], nbuf.at[to, unit]
        else:
            to = nz - 1
            part = pl.ds(0, q) if way == 0 else pl.ds(q, q)
            src, dst = nbuf.at[slot, unit, :, part], nbuf.at[to, unit, :, part]
        i = (s * half + h) * 2 + way
        return pltpu.make_async_remote_copy(
            src, dst, ring_send.at[i], ring_recv.at[i],
            device_id=(right if way == 0 else left, col), device_id_type=MESH,
        )

    swap_a = to_partner(n_ref.at[pl.ds(0, 8), pl.ds(other, kh)], nbuf.at[zero, ua], 0)
    swap_b = to_partner(bsend, brecv, 1)
    swap_p = to_partner(par.at[yh], par.at[yh], 2)
    ring(0, 0, 0).start()
    ring(0, 0, 1).start()
    swap_a.start()
    swap_b.start()
    swap_p.start()
    swap_f = [
        pltpu.make_async_remote_copy(
            f_ref.at[pl.ds(i * 32, 32), pl.ds(other, kh)], frecv.at[pl.ds(i * 32, 32)],
            fx_send.at[i], fx_recv.at[i], device_id=(partner, col), device_id_type=MESH,
        )
        for i in range(4)
    ]
    for c in swap_f:
        c.start()

    sites = f_ref.shape[0]

    def split_f(src, base, i):
        @pl.loop(0, 4)
        def _(j):
            hi, lo = split_bf16(src[pl.ds(pl.multiple_of(i * 32, 32), 32), pl.ds(pl.multiple_of(j * (kh // 4), kh // 4), kh // 4)])
            at = pl.ds(pl.multiple_of(base + i * 32, 32), 32)
            cols = pl.ds(pl.multiple_of(j * (kh // 4), kh // 4), kh // 4)
            fh[at, cols] = hi
            fl[at, cols] = lo

    def build_t1():
        swap_b.wait_recv()
        for j in range(2):
            own = nown[8:12, pl.ds(pl.multiple_of(mine + j * q, q), q)]
            got = brecv[4 * j : 4 * j + 4, :]
            both = jnp.concatenate([own, got], axis=0)
            flip = jnp.concatenate([got, own], axis=0)
            nbuf[zero, 1, :, j * q : (j + 1) * q] = jnp.where(yh == 0, both, flip)

    def build_onehot():
        ids = jnp.concatenate([par[0], par[1]], axis=1)[4:5, :]
        ids = jnp.broadcast_to(ids, (128, 2 * sites))
        ids = ids.T

        @pl.loop(0, plants // 128)
        def _(j):
            lane = lax.broadcasted_iota(jnp.int32, (2 * sites, 128), 1) + j * 128
            onehot[j] = jnp.where(ids == lane.astype(jnp.float32), 1.0, 0.0).astype(jnp.bfloat16)

    def matmul(slots, k_from, k_to, first):
        step = kh // 4
        m = 24 * len(slots)

        @pl.loop(k_from, k_to)
        def _(k):
            cols = pl.ds(pl.multiple_of(k * step, step), step)
            x = jnp.concatenate([nbuf[s, :, :, cols].reshape(24, step) for s in slots], axis=0)
            hi, lo = split_bf16(x)
            a, b = fh[:, cols], fl[:, cols]
            t = nt_dot(hi, a) + nt_dot(lo, a) + nt_dot(hi, b)

            @pl.when(k == 0)
            def _():
                acc[0:m, :] = t

            @pl.when(k != 0)
            def _():
                acc[0:m, :] += t

    def send_partials(slots):
        me = yh * nc + col
        for i, s in enumerate(slots):
            block = lax.rem(z + s - zero + nz, nz)
            t1 = acc[24 * i + 8 : 24 * i + 16, :]
            for y in range(2):
                a = acc[24 * i + 16 * y : 24 * i + 16 * y + 8, :]
                b = t1[4 * y : 4 * y + 4, :]
                b = jnp.concatenate([b[:, 0:128], b[:, 128:256]], axis=0)
                msg = jnp.concatenate([a, b], axis=1)
                self_ = jnp.logical_and(block == col, yh == y)

                @pl.when(self_)
                def _():
                    rrecv[me] = msg

                @pl.when(jnp.logical_not(self_))
                def _():
                    rsend[2 * s + y] = msg
                    pltpu.make_async_remote_copy(
                        rsend.at[2 * s + y], rrecv.at[me], r_send, r_recv,
                        device_id=(z * 2 + y, block), device_id_type=MESH,
                    ).start()

    def finish_sites():
        pltpu.make_async_copy(rrecv.at[pl.ds(0, peers - 1)], rrecv.at[pl.ds(0, peers - 1)], r_recv).wait()
        tot = rrecv[0]
        for i in range(1, peers):
            tot = tot + rrecv[i]
        b = jnp.concatenate([tot[0:4, 256:384], tot[4:8, 256:384]], axis=1)
        samples = jnp.concatenate([tot[:, 0:256], b, b], axis=0)
        p = jnp.concatenate([par[0], par[1]], axis=1)
        speed = p[0:1] + p[1:2] * samples
        positive = jnp.maximum(speed, 0.0)
        wind = jnp.clip((positive * positive * positive - 27.0) / (1728.0 - 27.0), 0.0, 1.0)
        solar = jnp.clip(speed / 12.0, 0.0, 1.0)
        power = jnp.where(p[3:4] == 1.0, solar, wind) * p[2:3]
        p0, rest = power.astype(jnp.bfloat16), power
        rest = rest - p0.astype(jnp.float32)
        p1 = rest.astype(jnp.bfloat16)
        p2 = (rest - p1.astype(jnp.float32)).astype(jnp.bfloat16)
        pieces = jnp.concatenate([p0, p1, p2], axis=0)
        low = lax.broadcasted_iota(jnp.int32, (8, 128), 1) < 64

        for j in range(nz):
            t = jnp.dot(pieces, onehot[j], preferred_element_type=jnp.float32)
            t = t[0:16] + t[16:32] + t[32:48]
            a, c = t[0:8], t[8:16]
            msgs = jnp.where(low, a, pltpu.roll(c, 64, 1)), jnp.where(low, pltpu.roll(a, 64, 1), c)
            for y in range(2):
                zsend[2 * j + y] = msgs[y]

        @pl.loop(0, rows)
        def _(r):
            @pl.when(r == row)
            def _():
                zrecv[row] = zsend[r]

            @pl.when(r != row)
            def _():
                pltpu.make_async_remote_copy(
                    zsend.at[r], zrecv.at[row], z_send, z_recv, device_id=(r, col), device_id_type=MESH
                ).start()

    slots_a = list(range(zero - near, zero + near + 1))
    slots_b = [s for s in range(nz) if s not in slots_a]
    off = lax.rem(col - z + zero + nz, nz)
    is_a = jnp.logical_and(off >= slots_a[0], off <= slots_a[-1])

    def forward(s, h):
        if h >= 1:
            for way in range(2):
                ring(s, h - 1, way).wait_recv()
                ring(s, h, way).start()
        elif s:
            if s == 1:
                swap_a.wait_recv()
            else:
                build_t1()
            ring(s, 0, 0).start()
            ring(s, 0, 1).start()

    for t in range(1, half + LAG):
        for s in range(3):
            h = t if s == 0 else t - LAG
            if h < half:
                forward(s, h)
        if t == 1:
            load_f.wait()
        if 1 <= t <= 2:
            for i in range(2):
                split_f(fown, yh * sites, 2 * t - 2 + i)
        if t == 2:
            swap_p.wait_recv()
            build_onehot()
        if 3 <= t <= 6 and half == 8:
            swap_f[t - 3].wait_recv()
            split_f(frecv, (1 - yh) * sites, t - 3)
        if half != 8 and t == 1:
            for i in range(4):
                swap_f[i].wait_recv()
                split_f(frecv, (1 - yh) * sites, i)

    matmul(slots_a, 0, 4, True)
    send_partials(slots_a)

    @pl.when(is_a)
    def _():
        finish_sites()

    for s in range(3):
        for way in range(2):
            ring(s, half - 1, way).wait_recv()
    matmul(slots_b, 0, 4, True)
    send_partials(slots_b)

    @pl.when(jnp.logical_not(is_a))
    def _():
        finish_sites()

    swap_a.wait_send()
    swap_b.wait_send()
    swap_p.wait_send()
    for c in swap_f:
        c.wait_send()
    for s in range(3):
        for h in range(half):
            for way in range(2):
                ring(s, h, way).wait_send()
    pltpu.make_async_copy(rsend.at[pl.ds(0, peers - 1)], rsend.at[pl.ds(0, peers - 1)], r_send).wait()
    pltpu.make_async_copy(zsend.at[pl.ds(0, rows - 1)], zsend.at[pl.ds(0, rows - 1)], z_send).wait()
    pltpu.make_async_copy(zrecv.at[pl.ds(0, rows - 1)], zrecv.at[pl.ds(0, rows - 1)], z_recv).wait()
    s0, s1 = zrecv[0], zrecv[1]
    for i in range(1, nz):
        s0 = s0 + zrecv[2 * i]
        s1 = s1 + zrecv[2 * i + 1]
    out_ref[0:8, :] = s0[:, 0:64]
    out_ref[8:12, :] = s0[0:4, 64:128]
    out_ref[12:20, :] = s1[:, 0:64]
    out_ref[20:24, :] = s1[0:4, 64:128]


def body(factor_band, normals, site_mean, site_spread, site_capacity, site_kind, site_plant):
    rows, nc = lax.axis_size("row"), lax.axis_size("col")
    nz = rows // 2
    half = nz // 2
    sites, k = factor_band.shape
    kh = k // 2
    plants = 64 * rows
    f32, bf16 = jnp.float32, jnp.bfloat16
    vmem = pl.BlockSpec(memory_space=pltpu.VMEM)
    hbm = pl.BlockSpec(memory_space=pl.ANY)
    dma = pltpu.SemaphoreType.DMA
    return pl.pallas_call(
        functools.partial(kernel, nz, nc, kh, plants),
        out_shape=jax.ShapeDtypeStruct((24, 64), f32),
        in_specs=[hbm, hbm] + [vmem] * 5,
        out_specs=vmem,
        scratch_shapes=[
            pltpu.VMEM((12, k), f32),
            pltpu.VMEM((nz, 3, 8, kh), f32),
            pltpu.VMEM((8, kh // 2), f32),
            pltpu.VMEM((8, kh // 2), f32),
            pltpu.VMEM((sites, kh), f32),
            pltpu.VMEM((sites, kh), f32),
            pltpu.VMEM((2 * sites, kh), bf16),
            pltpu.VMEM((2 * sites, kh), bf16),
            pltpu.VMEM((2, 8, 128), f32),
            pltpu.VMEM((nz, 2 * sites, 128), bf16),
            pltpu.VMEM((24 * (nz - 3), 2 * sites), f32),
            pltpu.VMEM((2 * nc, 8, 384), f32),
            pltpu.VMEM((2 * nc, 8, 384), f32),
            pltpu.VMEM((rows, 8, 128), f32),
            pltpu.VMEM((rows, 8, 128), f32),
            dma((3,)), dma((3,)), dma((3,)), dma((4,)), dma((4,)),
            dma((6 * half,)), dma((6 * half,)),
            dma, dma, dma, dma,
        ],
        compiler_params=pltpu.CompilerParams(
            collective_id=0, has_side_effects=True, vmem_limit_bytes=48 * 1024 * 1024
        ),
        cost_estimate=pl.CostEstimate(flops=3 * 2 * 24 * nz * 2 * sites * kh, bytes_accessed=4 * sites * k, transcendentals=0),
        name="band_to_plants",
    )(factor_band, normals.T, site_mean, site_spread, site_capacity, site_kind, site_plant)


def solution(mesh):
    in_specs = (P("row", "col"), P("col", "row"), P("row"), P("row"), P("row"), P("row"), P("row"))
    return jax.shard_map(body, mesh=mesh, in_specs=in_specs, out_specs=P("col", "row"), check_vma=False)
```

```python
import functools

import jax
import jax.numpy as jnp
from jax import lax
from jax.experimental import pallas as pl
from jax.experimental.pallas import tpu as pltpu
from jax.sharding import PartitionSpec as P

MESH = pl.DeviceIdType.MESH


def split_bf16(v):
    hi = v.astype(jnp.bfloat16)
    return hi, (v - hi.astype(jnp.float32)).astype(jnp.bfloat16)


def nt_dot(a, b):
    return lax.dot_general(a, b, (((1,), (1,)), ((), ())), preferred_element_type=jnp.float32)


def kernel(
    nz, nc, kh, plants,
    f_ref, n_ref, mean_ref, spread_ref, cap_ref, kind_ref, plant_ref, out_ref,
    sitef, sitei, nown, nbuf, bsend, brecv, fown, frecv, fh, fl, par, onehot, acc, rsend, rrecv, zsend, zrecv,
    loc_sem, nx_send, nx_recv, fx_send, fx_recv, ring_send, ring_recv, r_send, r_recv, z_send, z_recv,
):
    half = nz // 2
    zero = half - 1
    near = half - 2
    peers = 2 * nc
    rows = 2 * nz
    row, col = lax.axis_index("row"), lax.axis_index("col")
    z, yh = row // 2, lax.rem(row, 2)
    partner = row + 1 - 2 * yh
    right = lax.rem(z + 1, nz) * 2 + yh
    left = lax.rem(z + nz - 1, nz) * 2 + yh
    mine = pl.multiple_of(yh * kh, kh)
    other = pl.multiple_of((1 - yh) * kh, kh)
    ua, up = 2 * yh, 2 - 2 * yh

    barrier = pltpu.get_barrier_semaphore()
    for r in (right, left):
        pl.semaphore_signal(barrier, inc=1, device_id=(r, col), device_id_type=MESH)

    @pl.loop(0, peers)
    def _(i):
        r, c = z * 2 + i // nc, lax.rem(i, nc)

        @pl.when(jnp.logical_or(r != row, c != col))
        def _():
            pl.semaphore_signal(barrier, inc=1, device_id=(r, c), device_id_type=MESH)

    load_a = pltpu.make_async_copy(n_ref.at[pl.ds(0, 8), pl.ds(mine, kh)], nbuf.at[zero, ua], loc_sem.at[0])
    load_n = pltpu.make_async_copy(n_ref, nown, loc_sem.at[1])
    load_f = pltpu.make_async_copy(f_ref.at[:, pl.ds(mine, kh)], fown, loc_sem.at[2])
    floats, ints = (mean_ref, spread_ref, cap_ref), (kind_ref, plant_ref)
    load_s = [pltpu.make_async_copy(r, sitef.at[i], loc_sem.at[3 + i]) for i, r in enumerate(floats)]
    load_s += [pltpu.make_async_copy(r, sitei.at[i], loc_sem.at[6 + i]) for i, r in enumerate(ints)]
    load_n.start()
    load_a.start()
    for c in load_s:
        c.start()
    load_f.start()

    row_of = lax.broadcasted_iota(jnp.int32, (8, 128), 0)
    packed = jnp.zeros((8, 128), jnp.float32)
    for c in load_s:
        c.wait()
    for i in range(5):
        v = sitef[i : i + 1, :] if i < 3 else sitei[i - 3 : i - 2, :].astype(jnp.float32)
        packed = jnp.where(row_of == i, v, packed)
    par[yh] = packed
    load_n.wait()
    q = kh // 2
    bsend[0:4, :] = nown[8:12, pl.ds(other, q)]
    bsend[4:8, :] = nown[8:12, pl.ds(pl.multiple_of(other + q, q), q)]
    load_a.wait()

    pl.semaphore_wait(barrier, peers - 1 + 2)

    def to_partner(src, dst, i):
        return pltpu.make_async_remote_copy(
            src, dst, nx_send.at[i], nx_recv.at[i], device_id=(partner, col), device_id_type=MESH
        )

    def ring(s, h, way):
        unit = (ua, up, 1)[s]
        slot = zero - h if way == 0 else zero + h
        to = slot - 1 if way == 0 else slot + 1
        if h < half - 1:
            src, dst = nbuf.at[slot, unit], nbuf.at[to, unit]
        else:
            to = nz - 1
            part = pl.ds(0, q) if way == 0 else pl.ds(q, q)
            src, dst = nbuf.at[slot, unit, :, part], nbuf.at[to, unit, :, part]
        i = (s * half + h) * 2 + way
        return pltpu.make_async_remote_copy(
            src, dst, ring_send.at[i], ring_recv.at[i],
            device_id=(right if way == 0 else left, col), device_id_type=MESH,
        )

    swap_a = to_partner(n_ref.at[pl.ds(0, 8), pl.ds(other, kh)], nbuf.at[zero, ua], 0)
    swap_b = to_partner(bsend, brecv, 1)
    swap_p = to_partner(par.at[yh], par.at[yh], 2)
    ring(0, 0, 0).start()
    ring(0, 0, 1).start()
    swap_a.start()
    swap_b.start()
    swap_p.start()
    swap_f = [
        pltpu.make_async_remote_copy(
            f_ref.at[pl.ds(i * 32, 32), pl.ds(other, kh)], frecv.at[pl.ds(i * 32, 32)],
            fx_send.at[i], fx_recv.at[i], device_id=(partner, col), device_id_type=MESH,
        )
        for i in range(4)
    ]
    for c in swap_f:
        c.start()

    sites = f_ref.shape[0]

    def split_f(src, base, i):
        @pl.loop(0, 4)
        def _(j):
            hi, lo = split_bf16(src[pl.ds(pl.multiple_of(i * 32, 32), 32), pl.ds(pl.multiple_of(j * (kh // 4), kh // 4), kh // 4)])
            at = pl.ds(pl.multiple_of(base + i * 32, 32), 32)
            cols = pl.ds(pl.multiple_of(j * (kh // 4), kh // 4), kh // 4)
            fh[at, cols] = hi
            fl[at, cols] = lo

    def build_t1():
        swap_b.wait_recv()
        for j in range(2):
            own = nown[8:12, pl.ds(pl.multiple_of(mine + j * q, q), q)]
            got = brecv[4 * j : 4 * j + 4, :]
            both = jnp.concatenate([own, got], axis=0)
            flip = jnp.concatenate([got, own], axis=0)
            nbuf[zero, 1, :, j * q : (j + 1) * q] = jnp.where(yh == 0, both, flip)

    def build_onehot():
        ids = jnp.concatenate([par[0], par[1]], axis=1)[4:5, :]
        ids = jnp.broadcast_to(ids, (128, 2 * sites))
        ids = ids.T

        @pl.loop(0, plants // 128)
        def _(j):
            lane = lax.broadcasted_iota(jnp.int32, (2 * sites, 128), 1) + j * 128
            onehot[:, pl.ds(pl.multiple_of(j * 128, 128), 128)] = jnp.where(ids == lane.astype(jnp.float32), 1.0, 0.0).astype(jnp.bfloat16)

    def matmul(slots, parts, k_from, k_to):
        step = kh // parts
        m = 24 * len(slots)

        @pl.loop(k_from, k_to)
        def _(k):
            cols = pl.ds(pl.multiple_of(k * step, step), step)
            x = jnp.concatenate([nbuf[s, :, :, cols].reshape(24, step) for s in slots], axis=0)
            hi = x.astype(jnp.bfloat16).astype(jnp.float32)
            hl = jnp.concatenate([hi, x - hi], axis=0).astype(jnp.bfloat16)
            t = nt_dot(hl, fh[:, cols])
            t = t[0:m] + t[m : 2 * m] + nt_dot(hl[0:m], fl[:, cols])

            @pl.when(k == 0)
            def _():
                acc[0:m, :] = t

            @pl.when(k != 0)
            def _():
                acc[0:m, :] += t

    def send_partials(slots, first=0):
        me = yh * nc + col
        for i, s in enumerate(slots, first):
            block = lax.rem(z + s - zero + nz, nz)
            t1 = acc[24 * i + 8 : 24 * i + 16, :]
            for y in range(2):
                a = acc[24 * i + 16 * y : 24 * i + 16 * y + 8, :]
                b = t1[4 * y : 4 * y + 4, :]
                b = jnp.concatenate([b[:, 0:128], b[:, 128:256]], axis=0)
                msg = jnp.concatenate([a, b], axis=1)
                self_ = jnp.logical_and(block == col, yh == y)

                @pl.when(self_)
                def _():
                    rrecv[me] = msg

                @pl.when(jnp.logical_not(self_))
                def _():
                    rsend[2 * s + y] = msg
                    pltpu.make_async_remote_copy(
                        rsend.at[2 * s + y], rrecv.at[me], r_send, r_recv,
                        device_id=(z * 2 + y, block), device_id_type=MESH,
                    ).start()

    def finish_sites():
        pltpu.make_async_copy(rrecv.at[pl.ds(0, peers - 1)], rrecv.at[pl.ds(0, peers - 1)], r_recv).wait()
        tot = rrecv[0]
        for i in range(1, peers):
            tot = tot + rrecv[i]
        b = jnp.concatenate([tot[0:4, 256:384], tot[4:8, 256:384]], axis=1)
        samples = jnp.concatenate([tot[:, 0:256], b, b], axis=0)
        p = jnp.concatenate([par[0], par[1]], axis=1)
        speed = p[0:1] + p[1:2] * samples
        positive = jnp.maximum(speed, 0.0)
        wind = jnp.clip((positive * positive * positive - 27.0) / (1728.0 - 27.0), 0.0, 1.0)
        solar = jnp.clip(speed / 12.0, 0.0, 1.0)
        power = jnp.where(p[3:4] == 1.0, solar, wind) * p[2:3]
        p0, rest = power.astype(jnp.bfloat16), power
        rest = rest - p0.astype(jnp.float32)
        p1 = rest.astype(jnp.bfloat16)
        p2 = (rest - p1.astype(jnp.float32)).astype(jnp.bfloat16)
        pieces = jnp.concatenate([p0, p1, p2], axis=0)
        low = lax.broadcasted_iota(jnp.int32, (8, 128), 1) < 64

        sums = jnp.dot(pieces, onehot[...], preferred_element_type=jnp.float32)
        sums = sums[0:16] + sums[16:32] + sums[32:48]
        for j in range(nz):
            a, c = sums[0:8, 128 * j : 128 * (j + 1)], sums[8:16, 128 * j : 128 * (j + 1)]
            msgs = jnp.where(low, a, pltpu.roll(c, 64, 1)), jnp.where(low, pltpu.roll(a, 64, 1), c)
            for y in range(2):
                zsend[2 * j + y] = msgs[y]

        zrecv[row] = zsend[row]

        @pl.loop(0, rows - 1)
        def _(i):
            k = i // 2
            away = half + (k + 1) // 2 * (2 * lax.rem(k, 2) - 1)
            r = jnp.where(i < rows - 2, lax.rem(z + away, nz) * 2 + lax.rem(i, 2), partner)
            pltpu.make_async_remote_copy(
                zsend.at[r], zrecv.at[row], z_send, z_recv, device_id=(r, col), device_id_type=MESH
            ).start()

    slots_a = list(range(zero - near, zero + near + 1))
    slots_b = [0, nz - 2]

    def forward(s, h):
        if h >= 1:
            for way in range(2):
                ring(s, h - 1, way).wait_recv()
                ring(s, h, way).start()
        else:
            if s == 1:
                swap_a.wait_recv()
            else:
                build_t1()
            ring(s, 0, 0).start()
            ring(s, 0, 1).start()

    forward(0, 1)
    load_f.wait()
    for h in range(near):
        forward(1, h)
        forward(2, h)
        forward(0, h + 2)
        if h < 2:
            for i in range(2):
                split_f(fown, yh * sites, 2 * h + i)
        if h == min(2, near - 1):
            swap_p.wait_recv()
            build_onehot()
        for i in range(4):
            if h == max(near - 4 + i, 0):
                swap_f[i].wait_recv()
                split_f(frecv, (1 - yh) * sites, i)
    forward(1, near)
    forward(2, near)
    matmul(slots_a, 4, 0, 4)
    send_partials(slots_a[: near // 2])
    forward(1, near + 1)
    send_partials(slots_a[near // 2 :], near // 2)
    forward(2, near + 1)
    matmul(slots_b, 2, 0, 2)
    send_partials(slots_b)
    for s in range(3):
        for way in range(2):
            ring(s, half - 1, way).wait_recv()
    matmul([nz - 1], 2, 0, 2)
    send_partials([nz - 1])
    finish_sites()

    swap_a.wait_send()
    swap_b.wait_send()
    swap_p.wait_send()
    for c in swap_f:
        c.wait_send()
    for s in range(3):
        for h in range(half):
            for way in range(2):
                ring(s, h, way).wait_send()
    pltpu.make_async_copy(rsend.at[pl.ds(0, peers - 1)], rsend.at[pl.ds(0, peers - 1)], r_send).wait()
    pltpu.make_async_copy(zsend.at[pl.ds(0, rows - 1)], zsend.at[pl.ds(0, rows - 1)], z_send).wait()
    pltpu.make_async_copy(zrecv.at[pl.ds(0, rows - 1)], zrecv.at[pl.ds(0, rows - 1)], z_recv).wait()
    s0, s1 = zrecv[0], zrecv[1]
    for i in range(1, nz):
        s0 = s0 + zrecv[2 * i]
        s1 = s1 + zrecv[2 * i + 1]
    out_ref[0:8, :] = s0[:, 0:64]
    out_ref[8:12, :] = s0[0:4, 64:128]
    out_ref[12:20, :] = s1[:, 0:64]
    out_ref[20:24, :] = s1[0:4, 64:128]


def body(factor_band, normals, site_mean, site_spread, site_capacity, site_kind, site_plant):
    rows, nc = lax.axis_size("row"), lax.axis_size("col")
    nz = rows // 2
    half = nz // 2
    sites, k = factor_band.shape
    kh = k // 2
    plants = 64 * rows
    f32, bf16 = jnp.float32, jnp.bfloat16
    vmem = pl.BlockSpec(memory_space=pltpu.VMEM)
    hbm = pl.BlockSpec(memory_space=pl.ANY)
    dma = pltpu.SemaphoreType.DMA
    return pl.pallas_call(
        functools.partial(kernel, nz, nc, kh, plants),
        out_shape=jax.ShapeDtypeStruct((24, 64), f32),
        in_specs=[hbm] * 7,
        out_specs=vmem,
        scratch_shapes=[
            pltpu.VMEM((3, 128), f32),
            pltpu.VMEM((2, 128), jnp.int32),
            pltpu.VMEM((12, k), f32),
            pltpu.VMEM((nz, 3, 8, kh), f32),
            pltpu.VMEM((8, kh // 2), f32),
            pltpu.VMEM((8, kh // 2), f32),
            pltpu.VMEM((sites, kh), f32),
            pltpu.VMEM((sites, kh), f32),
            pltpu.VMEM((2 * sites, kh), bf16),
            pltpu.VMEM((2 * sites, kh), bf16),
            pltpu.VMEM((2, 8, 128), f32),
            pltpu.VMEM((2 * sites, plants), bf16),
            pltpu.VMEM((24 * (nz - 3), 2 * sites), f32),
            pltpu.VMEM((2 * nc, 8, 384), f32),
            pltpu.VMEM((2 * nc, 8, 384), f32),
            pltpu.VMEM((rows, 8, 128), f32),
            pltpu.VMEM((rows, 8, 128), f32),
            dma((8,)), dma((3,)), dma((3,)), dma((4,)), dma((4,)),
            dma((6 * half,)), dma((6 * half,)),
            dma, dma, dma, dma,
        ],
        compiler_params=pltpu.CompilerParams(
            collective_id=0, has_side_effects=True, vmem_limit_bytes=58 * 1024 * 1024
        ),
        cost_estimate=pl.CostEstimate(flops=3 * 2 * 24 * nz * 2 * sites * kh, bytes_accessed=4 * sites * k, transcendentals=0),
        name="band_to_plants",
    )(factor_band, normals.T, site_mean, site_spread, site_capacity, site_kind, site_plant)


def solution(mesh):
    in_specs = (P("row", "col"), P("col", "row"), P("row"), P("row"), P("row"), P("row"), P("row"))
    return jax.shard_map(body, mesh=mesh, in_specs=in_specs, out_specs=P("col", "row"), check_vma=False)
```

```python
import functools

import jax
import jax.numpy as jnp
from jax import lax
from jax.experimental import pallas as pl
from jax.experimental.pallas import tpu as pltpu
from jax.sharding import PartitionSpec as P

MESH = pl.DeviceIdType.MESH


def split_bf16(v):
    hi = v.astype(jnp.bfloat16)
    return hi, (v - hi.astype(jnp.float32)).astype(jnp.bfloat16)


def nt_dot(a, b):
    return lax.dot_general(a, b, (((1,), (1,)), ((), ())), preferred_element_type=jnp.float32)


def kernel(
    nz, nc, kh, plants,
    f_ref, n_ref, mean_ref, spread_ref, cap_ref, kind_ref, plant_ref, out_ref,
    sitef, sitei, nown, nbuf, bsend, brecv, fown, frecv, fh, fl, par, onehot, acc, rsend, rrecv, zsend, zrecv,
    loc_sem, nx_send, nx_recv, fx_send, fx_recv, ring_send, ring_recv, r_send, r_recv, z_send, z_recv, plane_sem, twin_sem,
):
    half = nz // 2
    zero = half - 1
    near = half - 2
    peers = 2 * nc
    rows = 2 * nz
    row, col = lax.axis_index("row"), lax.axis_index("col")
    z, yh = row // 2, lax.rem(row, 2)
    partner = row + 1 - 2 * yh
    right = lax.rem(z + 1, nz) * 2 + yh
    left = lax.rem(z + nz - 1, nz) * 2 + yh
    mine = pl.multiple_of(yh * kh, kh)
    other = pl.multiple_of((1 - yh) * kh, kh)
    ua, up = 2 * yh, 2 - 2 * yh

    barrier = pltpu.get_barrier_semaphore()
    for r in (right, left):
        pl.semaphore_signal(barrier, inc=1, device_id=(r, col), device_id_type=MESH)

    core, yl, x = lax.rem(col, 2), lax.rem(col // 2, 2), col // 4
    nx = nc // 4
    group = [(row, lax.rem(x + i, nx) * 4 + yl * 2 + core) for i in range(1, nx)]
    flipped = col + 2 - 4 * yl
    group += [(partner, col), (row, flipped), (partner, flipped)]
    twin = (row, col + 1 - 2 * core)

    def signal(sem, who):
        pl.semaphore_signal(sem, inc=1, device_id=who, device_id_type=MESH)

    for who in group:
        signal(barrier, who)

    @pl.when(core == 0)
    def _():
        signal(barrier, twin)

    load_a = pltpu.make_async_copy(n_ref.at[pl.ds(0, 8), pl.ds(mine, kh)], nbuf.at[zero, ua], loc_sem.at[0])
    load_n = pltpu.make_async_copy(n_ref, nown, loc_sem.at[1])
    load_f = pltpu.make_async_copy(f_ref.at[:, pl.ds(mine, kh)], fown, loc_sem.at[2])
    floats, ints = (mean_ref, spread_ref, cap_ref), (kind_ref, plant_ref)
    load_s = [pltpu.make_async_copy(r, sitef.at[i], loc_sem.at[3 + i]) for i, r in enumerate(floats)]
    load_s += [pltpu.make_async_copy(r, sitei.at[i], loc_sem.at[6 + i]) for i, r in enumerate(ints)]
    load_n.start()
    load_a.start()
    for c in load_s:
        c.start()
    load_f.start()

    def to_partner(src, dst, i):
        return pltpu.make_async_remote_copy(
            src, dst, nx_send.at[i], nx_recv.at[i], device_id=(partner, col), device_id_type=MESH
        )

    q = kh // 2

    def ring(s, h, way):
        unit = (ua, ua, up, 1)[s]
        slot = zero - h if way == 0 else zero + h
        to = slot - 1 if way == 0 else slot + 1
        if s < 2:
            part = pl.ds(s * q, q)
        else:
            part = pl.ds(0, kh) if h < half - 1 else pl.ds(way * q, q)
        if h == half - 1:
            to = nz - 1
        src = nbuf.at[slot, unit, :, part]
        if s < 2 and h == 0:
            src = n_ref.at[pl.ds(0, 8), pl.ds(pl.multiple_of(mine + s * q, q), q)]
        i = (s * half + h) * 2 + way
        return pltpu.make_async_remote_copy(
            src, nbuf.at[to, unit, :, part], ring_send.at[i], ring_recv.at[i],
            device_id=(right if way == 0 else left, col), device_id_type=MESH,
        )

    def steps(s, h):
        return (s,) if s < 2 and h == half - 1 else (0, 1)

    pl.semaphore_wait(barrier, 2 + len(group) + core)
    for s in range(2):
        for way in range(2):
            ring(s, 0, way).start()

    swap_a = to_partner(n_ref.at[pl.ds(0, 8), pl.ds(other, kh)], nbuf.at[zero, ua], 0)
    swap_a.start()

    row_of = lax.broadcasted_iota(jnp.int32, (8, 128), 0)
    packed = jnp.zeros((8, 128), jnp.float32)
    for c in load_s:
        c.wait()
    for i in range(5):
        v = sitef[i : i + 1, :] if i < 3 else sitei[i - 3 : i - 2, :].astype(jnp.float32)
        packed = jnp.where(row_of == i, v, packed)
    par[yh] = packed
    load_n.wait()
    bsend[0:4, :] = nown[8:12, pl.ds(other, q)]
    bsend[4:8, :] = nown[8:12, pl.ds(pl.multiple_of(other + q, q), q)]
    swap_b = to_partner(bsend, brecv, 1)
    swap_p = to_partner(par.at[yh], par.at[yh], 2)
    swap_b.start()
    swap_p.start()
    swap_f = [
        pltpu.make_async_remote_copy(
            f_ref.at[pl.ds(i * 32, 32), pl.ds(other, kh)], frecv.at[pl.ds(i * 32, 32)],
            fx_send.at[i], fx_recv.at[i], device_id=(partner, col), device_id_type=MESH,
        )
        for i in range(4)
    ]
    for c in swap_f:
        c.start()

    sites = f_ref.shape[0]

    def split_f(src, base, i):
        @pl.loop(0, 4)
        def _(j):
            hi, lo = split_bf16(src[pl.ds(pl.multiple_of(i * 32, 32), 32), pl.ds(pl.multiple_of(j * (kh // 4), kh // 4), kh // 4)])
            at = pl.ds(pl.multiple_of(base + i * 32, 32), 32)
            cols = pl.ds(pl.multiple_of(j * (kh // 4), kh // 4), kh // 4)
            fh[at, cols] = hi
            fl[at, cols] = lo

    def build_t1():
        swap_b.wait_recv()
        for j in range(2):
            own = nown[8:12, pl.ds(pl.multiple_of(mine + j * q, q), q)]
            got = brecv[4 * j : 4 * j + 4, :]
            both = jnp.concatenate([own, got], axis=0)
            flip = jnp.concatenate([got, own], axis=0)
            nbuf[zero, 1, :, j * q : (j + 1) * q] = jnp.where(yh == 0, both, flip)

    def build_onehot():
        ids = jnp.concatenate([par[0], par[1]], axis=1)[4:5, :]
        ids = jnp.broadcast_to(ids, (128, 2 * sites))
        ids = ids.T

        @pl.loop(0, plants // 128)
        def _(j):
            lane = lax.broadcasted_iota(jnp.int32, (2 * sites, 128), 1) + j * 128
            onehot[:, pl.ds(pl.multiple_of(j * 128, 128), 128)] = jnp.where(ids == lane.astype(jnp.float32), 1.0, 0.0).astype(jnp.bfloat16)

    def matmul(slots, parts, k_from, k_to):
        step = kh // parts
        m = 24 * len(slots)

        @pl.loop(k_from, k_to)
        def _(k):
            cols = pl.ds(pl.multiple_of(k * step, step), step)
            x = jnp.concatenate([nbuf[s, :, :, cols].reshape(24, step) for s in slots], axis=0)
            hi = x.astype(jnp.bfloat16).astype(jnp.float32)
            hl = jnp.concatenate([hi, x - hi], axis=0).astype(jnp.bfloat16)
            t = nt_dot(hl, fh[:, cols])
            t = t[0:m] + t[m : 2 * m] + nt_dot(hl[0:m], fl[:, cols])

            @pl.when(k == 0)
            def _():
                acc[0:m, :] = t

            @pl.when(k != 0)
            def _():
                acc[0:m, :] += t

    def send_partials(slots, first=0):
        me = yh * nc + col
        for i, s in enumerate(slots, first):
            block = lax.rem(z + s - zero + nz, nz)
            t1 = acc[24 * i + 8 : 24 * i + 16, :]
            for y in range(2):
                a = acc[24 * i + 16 * y : 24 * i + 16 * y + 8, :]
                b = t1[4 * y : 4 * y + 4, :]
                b = jnp.concatenate([b[:, 0:128], b[:, 128:256]], axis=0)
                msg = jnp.concatenate([a, b], axis=1)
                self_ = jnp.logical_and(block == col, yh == y)

                @pl.when(self_)
                def _():
                    rrecv[me] = msg

                @pl.when(jnp.logical_not(self_))
                def _():
                    rsend[2 * s + y] = msg
                    pltpu.make_async_remote_copy(
                        rsend.at[2 * s + y], rrecv.at[me], r_send, r_recv,
                        device_id=(z * 2 + y, block), device_id_type=MESH,
                    ).start()

    def finish_sites():
        pltpu.make_async_copy(rrecv.at[pl.ds(0, peers - 1)], rrecv.at[pl.ds(0, peers - 1)], r_recv).wait()
        tot = rrecv[0]
        for i in range(1, peers):
            tot = tot + rrecv[i]
        b = jnp.concatenate([tot[0:4, 256:384], tot[4:8, 256:384]], axis=1)
        a = tot[:, 0:256]
        samples = jnp.concatenate([a, a[6:8], b, b[0:2]], axis=0)
        p = jnp.concatenate([par[0], par[1]], axis=1)
        speed = p[0:1] + p[1:2] * samples
        positive = jnp.maximum(speed, 0.0)
        wind = jnp.clip((positive * positive * positive - 27.0) / (1728.0 - 27.0), 0.0, 1.0)
        solar = jnp.clip(speed / 12.0, 0.0, 1.0)
        power = jnp.where(p[3:4] == 1.0, solar, wind) * p[2:3]
        p0, rest = power.astype(jnp.bfloat16), power
        rest = rest - p0.astype(jnp.float32)
        p1 = rest.astype(jnp.bfloat16)
        p2 = (rest - p1.astype(jnp.float32)).astype(jnp.bfloat16)
        pieces = jnp.concatenate([p0, p1, p2], axis=0)
        low = lax.broadcasted_iota(jnp.int32, (8, 128), 1) < 64

        sums = jnp.dot(pieces, onehot[...], preferred_element_type=jnp.float32)
        sums = sums[0:16] + sums[16:32] + sums[32:48]
        for j in range(nz):
            a, c = sums[0:8, 128 * j : 128 * (j + 1)], sums[8:16, 128 * j : 128 * (j + 1)]
            msgs = jnp.where(low, a, pltpu.roll(c, 64, 1)), jnp.where(low, pltpu.roll(a, 64, 1), c)
            for y in range(2):
                zsend[2 * j + y] = msgs[y][0:6]

        zrecv[row] = zsend[row]

        @pl.loop(0, rows - 1)
        def _(i):
            k = i // 2
            away = half + (k + 1) // 2 * (2 * lax.rem(k, 2) - 1)
            r = jnp.where(i < rows - 2, lax.rem(z + away, nz) * 2 + lax.rem(i, 2), partner)
            pltpu.make_async_remote_copy(
                zsend.at[r], zrecv.at[row], z_send, z_recv, device_id=(r, col), device_id_type=MESH
            ).start()

    slots_a = list(range(zero - near, zero + near + 1))
    slots_b = [0, nz - 2]

    def forward(s, h):
        if h == 0 and s == 2:
            swap_a.wait_recv()
        if h == 0 and s == 3:
            build_t1()
        for way in range(2):
            if h:
                ring(s, h - 1, way).wait_recv()
            if way in steps(s, h):
                ring(s, h, way).start()

    for who in group:
        signal(plane_sem, who)

    @pl.when(core == 1)
    def _():
        signal(plane_sem, twin)

    forward(0, 1)
    forward(1, 1)
    load_f.wait()
    load_a.wait()
    pl.semaphore_wait(plane_sem, len(group) + 1 - core)
    signal(twin_sem, twin)
    for h in range(near):
        forward(2, h)
        forward(3, h)
        forward(0, h + 2)
        forward(1, h + 2)
        if h < 2:
            for i in range(2):
                split_f(fown, yh * sites, 2 * h + i)
        if h == min(2, near - 1):
            swap_p.wait_recv()
            build_onehot()
        for i in range(4):
            if h == max(near - 4 + i, 0):
                swap_f[i].wait_recv()
                split_f(frecv, (1 - yh) * sites, i)
    forward(2, near)
    forward(3, near)
    pl.semaphore_wait(twin_sem, 1)
    matmul(slots_a, 2, 0, 2)
    send_partials(slots_a[: near // 2])
    forward(2, near + 1)
    send_partials(slots_a[near // 2 :], near // 2)
    forward(3, near + 1)
    matmul(slots_b, 1, 0, 1)
    send_partials(slots_b)
    for s in range(4):
        for way in steps(s, half - 1):
            ring(s, half - 1, way).wait_recv()
    matmul([nz - 1], 2, 0, 2)
    send_partials([nz - 1])
    finish_sites()

    swap_a.wait_send()
    swap_b.wait_send()
    swap_p.wait_send()
    for c in swap_f:
        c.wait_send()
    for s in range(4):
        for h in range(half):
            for way in steps(s, h):
                ring(s, h, way).wait_send()
    pltpu.make_async_copy(rsend.at[pl.ds(0, peers - 1)], rsend.at[pl.ds(0, peers - 1)], r_send).wait()
    pltpu.make_async_copy(zsend.at[pl.ds(0, rows - 1)], zsend.at[pl.ds(0, rows - 1)], z_send).wait()
    pltpu.make_async_copy(zrecv.at[pl.ds(0, rows - 1)], zrecv.at[pl.ds(0, rows - 1)], z_recv).wait()
    s0, s1 = zrecv[0], zrecv[1]
    for i in range(1, nz):
        s0 = s0 + zrecv[2 * i]
        s1 = s1 + zrecv[2 * i + 1]
    out_ref[...] = jnp.concatenate([s0[:, 0:64], s0[:, 64:128], s1[:, 0:64], s1[:, 64:128]], axis=0)


def body(factor_band, normals, site_mean, site_spread, site_capacity, site_kind, site_plant):
    rows, nc = lax.axis_size("row"), lax.axis_size("col")
    nz = rows // 2
    half = nz // 2
    sites, k = factor_band.shape
    kh = k // 2
    plants = 64 * rows
    f32, bf16 = jnp.float32, jnp.bfloat16
    vmem = pl.BlockSpec(memory_space=pltpu.VMEM)
    hbm = pl.BlockSpec(memory_space=pl.ANY)
    dma = pltpu.SemaphoreType.DMA
    return pl.pallas_call(
        functools.partial(kernel, nz, nc, kh, plants),
        out_shape=jax.ShapeDtypeStruct((24, 64), f32),
        in_specs=[hbm] * 7,
        out_specs=vmem,
        scratch_shapes=[
            pltpu.VMEM((3, 128), f32),
            pltpu.VMEM((2, 128), jnp.int32),
            pltpu.VMEM((12, k), f32),
            pltpu.VMEM((nz, 3, 8, kh), f32),
            pltpu.VMEM((8, kh // 2), f32),
            pltpu.VMEM((8, kh // 2), f32),
            pltpu.VMEM((sites, kh), f32),
            pltpu.VMEM((sites, kh), f32),
            pltpu.VMEM((2 * sites, kh), bf16),
            pltpu.VMEM((2 * sites, kh), bf16),
            pltpu.VMEM((2, 8, 128), f32),
            pltpu.VMEM((2 * sites, plants), bf16),
            pltpu.VMEM((24 * (nz - 3), 2 * sites), f32),
            pltpu.VMEM((2 * nc, 8, 384), f32),
            pltpu.VMEM((2 * nc, 8, 384), f32),
            pltpu.VMEM((rows, 6, 128), f32),
            pltpu.VMEM((rows, 6, 128), f32),
            dma((8,)), dma((3,)), dma((3,)), dma((4,)), dma((4,)),
            dma((8 * half,)), dma((8 * half,)),
            dma, dma, dma, dma,
            pltpu.SemaphoreType.REGULAR, pltpu.SemaphoreType.REGULAR,
        ],
        compiler_params=pltpu.CompilerParams(
            collective_id=0, has_side_effects=True, vmem_limit_bytes=58 * 1024 * 1024
        ),
        cost_estimate=pl.CostEstimate(flops=3 * 2 * 24 * nz * 2 * sites * kh, bytes_accessed=4 * sites * k, transcendentals=0),
        name="band_to_plants",
    )(factor_band, normals.T, site_mean, site_spread, site_capacity, site_kind, site_plant)


def solution(mesh):
    in_specs = (P("row", "col"), P("col", "row"), P("row"), P("row"), P("row"), P("row"), P("row"))
    return jax.shard_map(body, mesh=mesh, in_specs=in_specs, out_specs=P("col", "row"), check_vma=False)
```

```python
import functools

import jax
import jax.numpy as jnp
from jax import lax
from jax.experimental import pallas as pl
from jax.experimental.pallas import tpu as pltpu
from jax.sharding import PartitionSpec as P

MESH = pl.DeviceIdType.MESH


def split_bf16(v):
    hi = v.astype(jnp.bfloat16)
    return hi, (v - hi.astype(jnp.float32)).astype(jnp.bfloat16)


def nt_dot(a, b):
    return lax.dot_general(a, b, (((1,), (1,)), ((), ())), preferred_element_type=jnp.float32)


def kernel(
    nz, nc, kh, plants,
    f_ref, n_ref, mean_ref, spread_ref, cap_ref, kind_ref, plant_ref, out_ref,
    sitef, sitei, nown, nbuf, bsend, brecv, fown, frecv, fh, fl, par, onehot, acc, rsend, rrecv, zsend, zrecv,
    loc_sem, nx_send, nx_recv, fx_send, fx_recv, ring_send, ring_recv, r_send, r_recv, z_send, z_recv, plane_sem, twin_sem,
):
    half = nz // 2
    zero = half - 1
    near = half - 2
    peers = 2 * nc
    rows = 2 * nz
    row, col = lax.axis_index("row"), lax.axis_index("col")
    z, yh = row // 2, lax.rem(row, 2)
    partner = row + 1 - 2 * yh
    right = lax.rem(z + 1, nz) * 2 + yh
    left = lax.rem(z + nz - 1, nz) * 2 + yh
    mine = pl.multiple_of(yh * kh, kh)
    other = pl.multiple_of((1 - yh) * kh, kh)
    ua, up = 2 * yh, 2 - 2 * yh

    barrier = pltpu.get_barrier_semaphore()
    for r in (right, left):
        pl.semaphore_signal(barrier, inc=1, device_id=(r, col), device_id_type=MESH)

    core, yl, x = lax.rem(col, 2), lax.rem(col // 2, 2), col // 4
    nx = nc // 4
    group = [(row, lax.rem(x + i, nx) * 4 + yl * 2 + core) for i in range(1, nx)]
    flipped = col + 2 - 4 * yl
    group += [(partner, col), (row, flipped), (partner, flipped)]
    twin = (row, col + 1 - 2 * core)

    def signal(sem, who):
        pl.semaphore_signal(sem, inc=1, device_id=who, device_id_type=MESH)

    for who in group:
        signal(barrier, who)

    @pl.when(core == 0)
    def _():
        signal(barrier, twin)

    load_a = pltpu.make_async_copy(n_ref.at[pl.ds(0, 8), pl.ds(mine, kh)], nbuf.at[zero, ua], loc_sem.at[0])
    load_n = pltpu.make_async_copy(n_ref, nown, loc_sem.at[1])
    load_f = pltpu.make_async_copy(f_ref.at[:, pl.ds(mine, kh)], fown, loc_sem.at[2])
    floats, ints = (mean_ref, spread_ref, cap_ref), (kind_ref, plant_ref)
    load_s = [pltpu.make_async_copy(r, sitef.at[i], loc_sem.at[3 + i]) for i, r in enumerate(floats)]
    load_s += [pltpu.make_async_copy(r, sitei.at[i], loc_sem.at[6 + i]) for i, r in enumerate(ints)]
    load_n.start()
    load_a.start()
    for c in load_s:
        c.start()
    load_f.start()

    def to_partner(src, dst, i):
        return pltpu.make_async_remote_copy(
            src, dst, nx_send.at[i], nx_recv.at[i], device_id=(partner, col), device_id_type=MESH
        )

    q = kh // 2

    def ring(s, h, way):
        unit = (ua, ua, up, 1)[s]
        slot = zero - h if way == 0 else zero + h
        to = slot - 1 if way == 0 else slot + 1
        if s < 2:
            part = pl.ds(s * q, q)
        else:
            part = pl.ds(0, kh) if h < half - 1 else pl.ds(way * q, q)
        if h == half - 1:
            to = nz - 1
        src = nbuf.at[slot, unit, :, part]
        if s < 2 and h == 0:
            src = n_ref.at[pl.ds(0, 8), pl.ds(pl.multiple_of(mine + s * q, q), q)]
        i = (s * half + h) * 2 + way
        return pltpu.make_async_remote_copy(
            src, nbuf.at[to, unit, :, part], ring_send.at[i], ring_recv.at[i],
            device_id=(right if way == 0 else left, col), device_id_type=MESH,
        )

    def steps(s, h):
        return (s,) if s < 2 and h == half - 1 else (0, 1)

    pl.semaphore_wait(barrier, 2 + len(group) + core)
    for s in range(2):
        for way in range(2):
            ring(s, 0, way).start()

    swap_a = to_partner(n_ref.at[pl.ds(0, 8), pl.ds(other, kh)], nbuf.at[zero, ua], 0)
    swap_a.start()

    row_of = lax.broadcasted_iota(jnp.int32, (8, 128), 0)
    packed = jnp.zeros((8, 128), jnp.float32)
    for c in load_s:
        c.wait()
    for i in range(5):
        v = sitef[i : i + 1, :] if i < 3 else sitei[i - 3 : i - 2, :].astype(jnp.float32)
        packed = jnp.where(row_of == i, v, packed)
    par[yh] = packed
    load_n.wait()
    bsend[0:4, :] = nown[8:12, pl.ds(other, q)]
    bsend[4:8, :] = nown[8:12, pl.ds(pl.multiple_of(other + q, q), q)]
    swap_b = to_partner(bsend, brecv, 1)
    swap_p = to_partner(par.at[yh], par.at[yh], 2)
    swap_b.start()
    swap_p.start()
    swap_f = [
        pltpu.make_async_remote_copy(
            f_ref.at[pl.ds(i * 32, 32), pl.ds(other, kh)], frecv.at[pl.ds(i * 32, 32)],
            fx_send.at[i], fx_recv.at[i], device_id=(partner, col), device_id_type=MESH,
        )
        for i in range(4)
    ]
    for c in swap_f:
        c.start()

    sites = f_ref.shape[0]

    def split_f(src, base, i):
        @pl.loop(0, 4)
        def _(j):
            hi, lo = split_bf16(src[pl.ds(pl.multiple_of(i * 32, 32), 32), pl.ds(pl.multiple_of(j * (kh // 4), kh // 4), kh // 4)])
            at = pl.ds(pl.multiple_of(base + i * 32, 32), 32)
            cols = pl.ds(pl.multiple_of(j * (kh // 4), kh // 4), kh // 4)
            fh[at, cols] = hi
            fl[at, cols] = lo

    def build_t1():
        swap_b.wait_recv()
        for j in range(2):
            own = nown[8:12, pl.ds(pl.multiple_of(mine + j * q, q), q)]
            got = brecv[4 * j : 4 * j + 4, :]
            both = jnp.concatenate([own, got], axis=0)
            flip = jnp.concatenate([got, own], axis=0)
            nbuf[zero, 1, :, j * q : (j + 1) * q] = jnp.where(yh == 0, both, flip)

    def build_onehot():
        ids = jnp.concatenate([par[0], par[1]], axis=1)[4:5, :]
        ids = jnp.broadcast_to(ids, (128, 2 * sites))
        ids = ids.T

        @pl.loop(0, plants // 128)
        def _(j):
            lane = lax.broadcasted_iota(jnp.int32, (2 * sites, 128), 1) + j * 128
            onehot[:, pl.ds(pl.multiple_of(j * 128, 128), 128)] = jnp.where(ids == lane.astype(jnp.float32), 1.0, 0.0).astype(jnp.bfloat16)

    def matmul(slots, parts, k_from, k_to):
        step = kh // parts
        m = 24 * len(slots)

        @pl.loop(k_from, k_to)
        def _(k):
            cols = pl.ds(pl.multiple_of(k * step, step), step)
            x = jnp.concatenate([nbuf[s, :, :, cols].reshape(24, step) for s in slots], axis=0)
            hi = x.astype(jnp.bfloat16).astype(jnp.float32)
            hl = jnp.concatenate([hi, x - hi], axis=0).astype(jnp.bfloat16)
            t = nt_dot(hl, fh[:, cols])
            t = t[0:m] + t[m : 2 * m] + nt_dot(hl[0:m], fl[:, cols])

            @pl.when(k == 0)
            def _():
                acc[0:m, :] = t

            @pl.when(k != 0)
            def _():
                acc[0:m, :] += t

    def send_partials(slots, first=0):
        me = yh * nc + col
        for i, s in enumerate(slots, first):
            block = lax.rem(z + s - zero + nz, nz)
            t1 = acc[24 * i + 8 : 24 * i + 16, :]
            for y in range(2):
                a = acc[24 * i + 16 * y : 24 * i + 16 * y + 8, :]
                b = t1[4 * y : 4 * y + 4, :]
                b = jnp.concatenate([b[:, 0:128], b[:, 128:256]], axis=0)
                msg = jnp.concatenate([a, b], axis=1)
                self_ = jnp.logical_and(block == col, yh == y)

                @pl.when(self_)
                def _():
                    rrecv[me] = msg

                @pl.when(jnp.logical_not(self_))
                def _():
                    rsend[2 * s + y] = msg
                    pltpu.make_async_remote_copy(
                        rsend.at[2 * s + y], rrecv.at[me], r_send, r_recv,
                        device_id=(z * 2 + y, block), device_id_type=MESH,
                    ).start()

    def finish_sites():
        pltpu.make_async_copy(rrecv.at[pl.ds(0, peers - 1)], rrecv.at[pl.ds(0, peers - 1)], r_recv).wait()
        tot = rrecv[0]
        for i in range(1, peers):
            tot = tot + rrecv[i]
        b = jnp.concatenate([tot[0:4, 256:384], tot[4:8, 256:384]], axis=1)
        a = tot[:, 0:256]
        samples = jnp.concatenate([a, a[6:8], b, b[0:2]], axis=0)
        p = jnp.concatenate([par[0], par[1]], axis=1)
        speed = p[0:1] + p[1:2] * samples
        positive = jnp.maximum(speed, 0.0)
        wind = jnp.clip((positive * positive * positive - 27.0) / (1728.0 - 27.0), 0.0, 1.0)
        solar = jnp.clip(speed / 12.0, 0.0, 1.0)
        power = jnp.where(p[3:4] == 1.0, solar, wind) * p[2:3]
        p0, rest = power.astype(jnp.bfloat16), power
        rest = rest - p0.astype(jnp.float32)
        p1 = rest.astype(jnp.bfloat16)
        p2 = (rest - p1.astype(jnp.float32)).astype(jnp.bfloat16)
        pieces = jnp.concatenate([p0, p1, p2], axis=0)
        low = lax.broadcasted_iota(jnp.int32, (8, 128), 1) < 64

        sums = jnp.dot(pieces, onehot[...], preferred_element_type=jnp.float32)
        sums = sums[0:16] + sums[16:32] + sums[32:48]
        for j in range(nz):
            a, c = sums[0:8, 128 * j : 128 * (j + 1)], sums[8:16, 128 * j : 128 * (j + 1)]
            msgs = jnp.where(low, a, pltpu.roll(c, 64, 1)), jnp.where(low, pltpu.roll(a, 64, 1), c)
            for y in range(2):
                zsend[2 * j + y] = msgs[y][0:6]

        zrecv[row] = zsend[row]

        @pl.loop(0, rows - 1)
        def _(i):
            k = i // 2
            away = half + (k + 1) // 2 * (2 * lax.rem(k, 2) - 1)
            r = jnp.where(i < rows - 2, lax.rem(z + away, nz) * 2 + lax.rem(i, 2), partner)
            pltpu.make_async_remote_copy(
                zsend.at[r], zrecv.at[row], z_send, z_recv, device_id=(r, col), device_id_type=MESH
            ).start()

    slots_a = list(range(zero - near, zero + near + 1))
    slots_b = [0, nz - 2]

    def forward(s, h):
        if h == 0 and s == 2:
            swap_a.wait_recv()
        if h == 0 and s == 3:
            build_t1()
        for way in range(2):
            if h:
                ring(s, h - 1, way).wait_recv()
            if way in steps(s, h):
                ring(s, h, way).start()

    for who in group:
        signal(plane_sem, who)

    @pl.when(core == 1)
    def _():
        signal(plane_sem, twin)

    forward(0, 1)
    forward(1, 1)
    load_f.wait()
    load_a.wait()
    pl.semaphore_wait(plane_sem, len(group) + 1 - core)
    signal(twin_sem, twin)
    for h in range(near):
        forward(2, h)
        forward(3, h)
        forward(0, h + 2)
        forward(1, h + 2)
        if h < 2:
            for i in range(2):
                split_f(fown, yh * sites, 2 * h + i)
        if h == min(2, near - 1):
            swap_p.wait_recv()
            build_onehot()
        for i in range(4):
            if h == max(near - 4 + i, 0):
                swap_f[i].wait_recv()
                split_f(frecv, (1 - yh) * sites, i)
    forward(2, near)
    forward(3, near)
    pl.semaphore_wait(twin_sem, 1)
    matmul(slots_a, 2, 0, 2)
    send_partials(slots_a[: near // 2])
    forward(2, near + 1)
    send_partials(slots_a[near // 2 :], near // 2)
    forward(3, near + 1)
    matmul(slots_b, 1, 0, 1)
    send_partials(slots_b)
    for s in range(4):
        for way in steps(s, half - 1):
            ring(s, half - 1, way).wait_recv()
    matmul([nz - 1], 2, 0, 2)
    send_partials([nz - 1])
    finish_sites()

    swap_a.wait_send()
    swap_b.wait_send()
    swap_p.wait_send()
    for c in swap_f:
        c.wait_send()
    for s in range(4):
        for h in range(half):
            for way in steps(s, h):
                ring(s, h, way).wait_send()
    pltpu.make_async_copy(rsend.at[pl.ds(0, peers - 1)], rsend.at[pl.ds(0, peers - 1)], r_send).wait()
    pltpu.make_async_copy(zsend.at[pl.ds(0, rows - 1)], zsend.at[pl.ds(0, rows - 1)], z_send).wait()
    pltpu.make_async_copy(zrecv.at[pl.ds(0, rows - 1)], zrecv.at[pl.ds(0, rows - 1)], z_recv).wait()
    s0, s1 = zrecv[0], zrecv[1]
    for i in range(1, nz):
        s0 = s0 + zrecv[2 * i]
        s1 = s1 + zrecv[2 * i + 1]
    out_ref[...] = jnp.concatenate([s0[:, 0:64], s0[:, 64:128], s1[:, 0:64], s1[:, 64:128]], axis=0)


def body(factor_band, normals, site_mean, site_spread, site_capacity, site_kind, site_plant):
    rows, nc = lax.axis_size("row"), lax.axis_size("col")
    nz = rows // 2
    half = nz // 2
    sites, k = factor_band.shape
    kh = k // 2
    plants = 64 * rows
    f32, bf16 = jnp.float32, jnp.bfloat16
    vmem = pl.BlockSpec(memory_space=pltpu.VMEM)
    hbm = pl.BlockSpec(memory_space=pltpu.HBM)
    dma = pltpu.SemaphoreType.DMA
    return pl.pallas_call(
        functools.partial(kernel, nz, nc, kh, plants),
        out_shape=pltpu.VMEM((24, 64), f32),
        in_specs=[hbm] * 7,
        out_specs=vmem,
        scratch_shapes=[
            pltpu.VMEM((3, 128), f32),
            pltpu.VMEM((2, 128), jnp.int32),
            pltpu.VMEM((12, k), f32),
            pltpu.VMEM((nz, 3, 8, kh), f32),
            pltpu.VMEM((8, kh // 2), f32),
            pltpu.VMEM((8, kh // 2), f32),
            pltpu.VMEM((sites, kh), f32),
            pltpu.VMEM((sites, kh), f32),
            pltpu.VMEM((2 * sites, kh), bf16),
            pltpu.VMEM((2 * sites, kh), bf16),
            pltpu.VMEM((2, 8, 128), f32),
            pltpu.VMEM((2 * sites, plants), bf16),
            pltpu.VMEM((24 * (nz - 3), 2 * sites), f32),
            pltpu.VMEM((2 * nc, 8, 384), f32),
            pltpu.VMEM((2 * nc, 8, 384), f32),
            pltpu.VMEM((rows, 6, 128), f32),
            pltpu.VMEM((rows, 6, 128), f32),
            dma((8,)), dma((3,)), dma((3,)), dma((4,)), dma((4,)),
            dma((8 * half,)), dma((8 * half,)),
            dma, dma, dma, dma,
            pltpu.SemaphoreType.REGULAR, pltpu.SemaphoreType.REGULAR,
        ],
        compiler_params=pltpu.CompilerParams(
            collective_id=0, has_side_effects=True, vmem_limit_bytes=48 * 1024 * 1024
        ),
        cost_estimate=pl.CostEstimate(flops=3 * 2 * 24 * nz * 2 * sites * kh, bytes_accessed=4 * sites * k, transcendentals=0),
        name="band_to_plants",
    )(*(pltpu.with_memory_space_constraint(v, pltpu.HBM) for v in (factor_band, normals.T, site_mean, site_spread, site_capacity, site_kind, site_plant)))


def solution(mesh):
    in_specs = (P("row", "col"), P("col", "row"), P("row"), P("row"), P("row"), P("row"), P("row"))
    return jax.shard_map(body, mesh=mesh, in_specs=in_specs, out_specs=P("col", "row"), check_vma=False)
```

```python
import functools

import jax
import jax.numpy as jnp
from jax import lax
from jax.experimental import pallas as pl
from jax.experimental.pallas import tpu as pltpu
from jax.sharding import PartitionSpec as P

MESH = pl.DeviceIdType.MESH


def split_bf16(v):
    hi = v.astype(jnp.bfloat16)
    return hi, (v - hi.astype(jnp.float32)).astype(jnp.bfloat16)


def nt_dot(a, b):
    return lax.dot_general(a, b, (((1,), (1,)), ((), ())), preferred_element_type=jnp.float32)


def kernel(
    nz, nc, kh, plants,
    f_ref, n_ref, mean_ref, spread_ref, cap_ref, kind_ref, plant_ref, out_ref,
    sitef, sitei, nown, nbuf, bsend, brecv, fown, frecv, fh, fl, par, onehot, acc, rsend, rrecv, zsend, zrecv,
    loc_sem, nx_send, nx_recv, fx_send, fx_recv, ring_send, ring_recv, r_send, r_recv, z_send, z_recv, plane_sem, twin_sem,
):
    half = nz // 2
    zero = half - 1
    near = half - 2
    peers = 2 * nc
    rows = 2 * nz
    row, col = lax.axis_index("row"), lax.axis_index("col")
    z, yh = row // 2, lax.rem(row, 2)
    partner = row + 1 - 2 * yh
    right = lax.rem(z + 1, nz) * 2 + yh
    left = lax.rem(z + nz - 1, nz) * 2 + yh
    mine = pl.multiple_of(yh * kh, kh)
    other = pl.multiple_of((1 - yh) * kh, kh)
    ua, up = 2 * yh, 2 - 2 * yh

    barrier = pltpu.get_barrier_semaphore()
    for r in (right, left):
        pl.semaphore_signal(barrier, inc=1, device_id=(r, col), device_id_type=MESH)

    core, yl, x = lax.rem(col, 2), lax.rem(col // 2, 2), col // 4
    nx = nc // 4
    group = [(row, lax.rem(x + i, nx) * 4 + yl * 2 + core) for i in range(1, nx)]
    flipped = col + 2 - 4 * yl
    group += [(partner, col), (row, flipped), (partner, flipped)]
    twin = (row, col + 1 - 2 * core)

    def signal(sem, who):
        pl.semaphore_signal(sem, inc=1, device_id=who, device_id_type=MESH)

    for who in group:
        signal(barrier, who)

    @pl.when(core == 0)
    def _():
        signal(barrier, twin)

    load_a = pltpu.make_async_copy(n_ref.at[pl.ds(0, 8), pl.ds(mine, kh)], nbuf.at[zero, ua], loc_sem.at[0])
    load_n = pltpu.make_async_copy(n_ref, nown, loc_sem.at[1])
    load_f = pltpu.make_async_copy(f_ref.at[:, pl.ds(mine, kh)], fown, loc_sem.at[2])
    floats, ints = (mean_ref, spread_ref, cap_ref), (kind_ref, plant_ref)
    load_s = [pltpu.make_async_copy(r, sitef.at[i], loc_sem.at[3 + i]) for i, r in enumerate(floats)]
    load_s += [pltpu.make_async_copy(r, sitei.at[i], loc_sem.at[6 + i]) for i, r in enumerate(ints)]
    load_n.start()
    load_a.start()
    for c in load_s:
        c.start()
    load_f.start()

    def to_partner(src, dst, i):
        return pltpu.make_async_remote_copy(
            src, dst, nx_send.at[i], nx_recv.at[i], device_id=(partner, col), device_id_type=MESH
        )

    q = kh // 2

    def ring(s, h, way):
        unit = (ua, ua, up, 1)[s]
        slot = zero - h if way == 0 else zero + h
        to = slot - 1 if way == 0 else slot + 1
        if s < 2:
            part = pl.ds(s * q, q)
        else:
            part = pl.ds(0, kh) if h < half - 1 else pl.ds(way * q, q)
        if h == half - 1:
            to = nz - 1
        src = nbuf.at[slot, unit, :, part]
        if s < 2 and h == 0:
            src = n_ref.at[pl.ds(0, 8), pl.ds(pl.multiple_of(mine + s * q, q), q)]
        i = (s * half + h) * 2 + way
        return pltpu.make_async_remote_copy(
            src, nbuf.at[to, unit, :, part], ring_send.at[i], ring_recv.at[i],
            device_id=(right if way == 0 else left, col), device_id_type=MESH,
        )

    def steps(s, h):
        return (s,) if s < 2 and h == half - 1 else (0, 1)

    pl.semaphore_wait(barrier, 2 + len(group) + core)
    for s in range(2):
        for way in range(2):
            ring(s, 0, way).start()

    swap_a = to_partner(n_ref.at[pl.ds(0, 8), pl.ds(other, kh)], nbuf.at[zero, ua], 0)
    swap_a.start()

    row_of = lax.broadcasted_iota(jnp.int32, (8, 128), 0)
    packed = jnp.zeros((8, 128), jnp.float32)
    for c in load_s:
        c.wait()
    for i in range(5):
        v = sitef[i : i + 1, :] if i < 3 else sitei[i - 3 : i - 2, :].astype(jnp.float32)
        packed = jnp.where(row_of == i, v, packed)
    par[yh] = packed
    load_n.wait()
    bsend[0:4, :] = nown[8:12, pl.ds(other, q)]
    bsend[4:8, :] = nown[8:12, pl.ds(pl.multiple_of(other + q, q), q)]
    swap_b = to_partner(bsend, brecv, 1)
    swap_p = to_partner(par.at[yh], par.at[yh], 2)
    swap_b.start()
    swap_p.start()
    swap_f = [
        pltpu.make_async_remote_copy(
            f_ref.at[pl.ds(i * 32, 32), pl.ds(other, kh)], frecv.at[pl.ds(i * 32, 32)],
            fx_send.at[i], fx_recv.at[i], device_id=(partner, col), device_id_type=MESH,
        )
        for i in range(4)
    ]
    for c in swap_f:
        c.start()

    sites = f_ref.shape[0]

    def split_f(src, base, i):
        @pl.loop(0, 4)
        def _(j):
            hi, lo = split_bf16(src[pl.ds(pl.multiple_of(i * 32, 32), 32), pl.ds(pl.multiple_of(j * (kh // 4), kh // 4), kh // 4)])
            at = pl.ds(pl.multiple_of(base + i * 32, 32), 32)
            cols = pl.ds(pl.multiple_of(j * (kh // 4), kh // 4), kh // 4)
            fh[at, cols] = hi
            fl[at, cols] = lo

    def build_t1():
        swap_b.wait_recv()
        for j in range(2):
            own = nown[8:12, pl.ds(pl.multiple_of(mine + j * q, q), q)]
            got = brecv[4 * j : 4 * j + 4, :]
            both = jnp.concatenate([own, got], axis=0)
            flip = jnp.concatenate([got, own], axis=0)
            nbuf[zero, 1, :, j * q : (j + 1) * q] = jnp.where(yh == 0, both, flip)

    def build_onehot():
        ids = jnp.concatenate([par[0], par[1]], axis=1)[4:5, :]
        ids = jnp.broadcast_to(ids, (128, 2 * sites))
        ids = ids.T

        @pl.loop(0, plants // 128)
        def _(j):
            lane = lax.broadcasted_iota(jnp.int32, (2 * sites, 128), 1) + j * 128
            onehot[:, pl.ds(pl.multiple_of(j * 128, 128), 128)] = jnp.where(ids == lane.astype(jnp.float32), 1.0, 0.0).astype(jnp.bfloat16)

    def matmul(slots, parts, k_from, k_to, units=()):
        step = kh // parts
        m = 24 * len(slots) + 8 * len(units)

        @pl.loop(k_from, k_to)
        def _(k):
            cols = pl.ds(pl.multiple_of(k * step, step), step)
            x = [nbuf[s, :, :, cols].reshape(24, step) for s in slots]
            x = jnp.concatenate(x + [nbuf[nz - 1, u, :, cols] for u in units], axis=0)
            hi = x.astype(jnp.bfloat16).astype(jnp.float32)
            hl = jnp.concatenate([hi, x - hi], axis=0).astype(jnp.bfloat16)
            t = nt_dot(hl, fh[:, cols])
            t = t[0:m] + t[m : 2 * m] + nt_dot(hl[0:m], fl[:, cols])

            @pl.when(k == 0)
            def _():
                acc[0:m, :] = t

            @pl.when(k != 0)
            def _():
                acc[0:m, :] += t

    def send_partials(slots, first=0):
        me = yh * nc + col
        for i, s in enumerate(slots, first):
            block = lax.rem(z + s - zero + nz, nz)
            t1 = acc[24 * i + 8 : 24 * i + 16, :]
            for y in range(2):
                a = acc[24 * i + 16 * y : 24 * i + 16 * y + 8, :]
                b = t1[4 * y : 4 * y + 4, :]
                b = jnp.concatenate([b[:, 0:128], b[:, 128:256]], axis=0)
                msg = jnp.concatenate([a, b], axis=1)
                self_ = jnp.logical_and(block == col, yh == y)

                @pl.when(self_)
                def _():
                    rrecv[me] = msg

                @pl.when(jnp.logical_not(self_))
                def _():
                    rsend[2 * s + y] = msg
                    pltpu.make_async_remote_copy(
                        rsend.at[2 * s + y], rrecv.at[me], r_send, r_recv,
                        device_id=(z * 2 + y, block), device_id_type=MESH,
                    ).start()

    def send_last(y, msg, lanes):
        me, block = yh * nc + col, lax.rem(z + half, nz)
        self_ = jnp.logical_and(block == col, yh == y)

        @pl.when(self_)
        def _():
            rrecv[me, :, lanes] = msg

        @pl.when(jnp.logical_not(self_))
        def _():
            i = 2 * (nz - 1) + y
            rsend[i, :, lanes] = msg
            pltpu.make_async_remote_copy(
                rsend.at[i, :, lanes], rrecv.at[me, :, lanes], r_send, r_recv,
                device_id=(z * 2 + y, block), device_id_type=MESH,
            ).start()

    def finish_sites():
        pltpu.make_async_copy(rrecv.at[pl.ds(0, peers - 1)], rrecv.at[pl.ds(0, peers - 1)], r_recv).wait()
        tot = rrecv[0]
        for i in range(1, peers):
            tot = tot + rrecv[i]
        b = jnp.concatenate([tot[0:4, 256:384], tot[4:8, 256:384]], axis=1)
        a = tot[:, 0:256]
        samples = jnp.concatenate([a, a[6:8], b, b[0:2]], axis=0)
        p = jnp.concatenate([par[0], par[1]], axis=1)
        speed = p[0:1] + p[1:2] * samples
        positive = jnp.maximum(speed, 0.0)
        wind = jnp.clip((positive * positive * positive - 27.0) / (1728.0 - 27.0), 0.0, 1.0)
        solar = jnp.clip(speed / 12.0, 0.0, 1.0)
        power = jnp.where(p[3:4] == 1.0, solar, wind) * p[2:3]
        p0, rest = power.astype(jnp.bfloat16), power
        rest = rest - p0.astype(jnp.float32)
        p1 = rest.astype(jnp.bfloat16)
        p2 = (rest - p1.astype(jnp.float32)).astype(jnp.bfloat16)
        pieces = jnp.concatenate([p0, p1, p2], axis=0)
        low = lax.broadcasted_iota(jnp.int32, (8, 128), 1) < 64

        sums = jnp.dot(pieces, onehot[...], preferred_element_type=jnp.float32)
        sums = sums[0:16] + sums[16:32] + sums[32:48]
        for j in range(nz):
            a, c = sums[0:8, 128 * j : 128 * (j + 1)], sums[8:16, 128 * j : 128 * (j + 1)]
            msgs = jnp.where(low, a, pltpu.roll(c, 64, 1)), jnp.where(low, pltpu.roll(a, 64, 1), c)
            for y in range(2):
                zsend[2 * j + y] = msgs[y][0:6]

        zrecv[row] = zsend[row]

        @pl.loop(0, rows - 1)
        def _(i):
            k = i // 2
            away = half + (k + 1) // 2 * (2 * lax.rem(k, 2) - 1)
            r = jnp.where(i < rows - 2, lax.rem(z + away, nz) * 2 + lax.rem(i, 2), partner)
            pltpu.make_async_remote_copy(
                zsend.at[r], zrecv.at[row], z_send, z_recv, device_id=(r, col), device_id_type=MESH
            ).start()

    slots_a = list(range(zero - near, zero + near + 1))
    slots_b = [0, nz - 2]

    def forward(s, h):
        if h == 0 and s == 2:
            swap_a.wait_recv()
        if h == 0 and s == 3:
            build_t1()
        for way in range(2):
            if h:
                ring(s, h - 1, way).wait_recv()
            if way in steps(s, h):
                ring(s, h, way).start()

    for who in group:
        signal(plane_sem, who)

    @pl.when(core == 1)
    def _():
        signal(plane_sem, twin)

    forward(0, 1)
    forward(1, 1)
    load_f.wait()
    load_a.wait()
    pl.semaphore_wait(plane_sem, len(group) + 1 - core)
    signal(twin_sem, twin)
    for h in range(near):
        forward(2, h)
        forward(3, h)
        forward(0, h + 2)
        forward(1, h + 2)
        if h < 2:
            for i in range(2):
                split_f(fown, yh * sites, 2 * h + i)
        if h == min(2, near - 1):
            swap_p.wait_recv()
            build_onehot()
        for i in range(4):
            if h == max(near - 4 + i, 0):
                swap_f[i].wait_recv()
                split_f(frecv, (1 - yh) * sites, i)
    forward(2, near)
    forward(3, near)
    pl.semaphore_wait(twin_sem, 1)
    matmul(slots_a, 2, 0, 2)
    send_partials(slots_a[: near // 2])
    forward(2, near + 1)
    send_partials(slots_a[near // 2 :], near // 2)
    forward(3, near + 1)
    for s in range(3):
        for way in steps(s, half - 1):
            ring(s, half - 1, way).wait_recv()
    matmul(slots_b, 1, 0, 1, (0, 2))
    for y in range(2):
        send_last(y, acc[48 + 8 * y : 56 + 8 * y, :], pl.ds(0, 256))
    send_partials(slots_b)
    for way in range(2):
        ring(3, half - 1, way).wait_recv()
    matmul([], 2, 0, 2, (1,))
    for y in range(2):
        b = acc[4 * y : 4 * y + 4, :]
        send_last(y, jnp.concatenate([b[:, 0:128], b[:, 128:256]], axis=0), pl.ds(256, 128))
    finish_sites()

    swap_a.wait_send()
    swap_b.wait_send()
    swap_p.wait_send()
    for c in swap_f:
        c.wait_send()
    for s in range(4):
        for h in range(half):
            for way in steps(s, h):
                ring(s, h, way).wait_send()
    pltpu.make_async_copy(rsend.at[pl.ds(0, peers - 1)], rsend.at[pl.ds(0, peers - 1)], r_send).wait()
    pltpu.make_async_copy(zsend.at[pl.ds(0, rows - 1)], zsend.at[pl.ds(0, rows - 1)], z_send).wait()
    pltpu.make_async_copy(zrecv.at[pl.ds(0, rows - 1)], zrecv.at[pl.ds(0, rows - 1)], z_recv).wait()
    s0, s1 = zrecv[0], zrecv[1]
    for i in range(1, nz):
        s0 = s0 + zrecv[2 * i]
        s1 = s1 + zrecv[2 * i + 1]
    out_ref[...] = jnp.concatenate([s0[:, 0:64], s0[:, 64:128], s1[:, 0:64], s1[:, 64:128]], axis=0)


def body(factor_band, normals, site_mean, site_spread, site_capacity, site_kind, site_plant):
    rows, nc = lax.axis_size("row"), lax.axis_size("col")
    nz = rows // 2
    half = nz // 2
    sites, k = factor_band.shape
    kh = k // 2
    plants = 64 * rows
    f32, bf16 = jnp.float32, jnp.bfloat16
    vmem = pl.BlockSpec(memory_space=pltpu.VMEM)
    hbm = pl.BlockSpec(memory_space=pltpu.HBM)
    dma = pltpu.SemaphoreType.DMA
    return pl.pallas_call(
        functools.partial(kernel, nz, nc, kh, plants),
        out_shape=pltpu.VMEM((24, 64), f32),
        in_specs=[hbm] * 7,
        out_specs=vmem,
        scratch_shapes=[
            pltpu.VMEM((3, 128), f32),
            pltpu.VMEM((2, 128), jnp.int32),
            pltpu.VMEM((12, k), f32),
            pltpu.VMEM((nz, 3, 8, kh), f32),
            pltpu.VMEM((8, kh // 2), f32),
            pltpu.VMEM((8, kh // 2), f32),
            pltpu.VMEM((sites, kh), f32),
            pltpu.VMEM((sites, kh), f32),
            pltpu.VMEM((2 * sites, kh), bf16),
            pltpu.VMEM((2 * sites, kh), bf16),
            pltpu.VMEM((2, 8, 128), f32),
            pltpu.VMEM((2 * sites, plants), bf16),
            pltpu.VMEM((24 * (nz - 3), 2 * sites), f32),
            pltpu.VMEM((2 * nc, 8, 384), f32),
            pltpu.VMEM((2 * nc, 8, 384), f32),
            pltpu.VMEM((rows, 6, 128), f32),
            pltpu.VMEM((rows, 6, 128), f32),
            dma((8,)), dma((3,)), dma((3,)), dma((4,)), dma((4,)),
            dma((8 * half,)), dma((8 * half,)),
            dma, dma, dma, dma,
            pltpu.SemaphoreType.REGULAR, pltpu.SemaphoreType.REGULAR,
        ],
        compiler_params=pltpu.CompilerParams(
            collective_id=0, has_side_effects=True, vmem_limit_bytes=48 * 1024 * 1024
        ),
        cost_estimate=pl.CostEstimate(flops=3 * 2 * 24 * nz * 2 * sites * kh, bytes_accessed=4 * sites * k, transcendentals=0),
        name="band_to_plants",
    )(*(pltpu.with_memory_space_constraint(v, pltpu.HBM) for v in (factor_band, normals.T, site_mean, site_spread, site_capacity, site_kind, site_plant)))


def solution(mesh):
    in_specs = (P("row", "col"), P("col", "row"), P("row"), P("row"), P("row"), P("row"), P("row"))
    return jax.shard_map(body, mesh=mesh, in_specs=in_specs, out_specs=P("col", "row"), check_vma=False)
```

```python
import functools

import jax
import jax.numpy as jnp
from jax import lax
from jax.experimental import pallas as pl
from jax.experimental.pallas import tpu as pltpu
from jax.sharding import PartitionSpec as P

MESH = pl.DeviceIdType.MESH


def split_bf16(v):
    hi = v.astype(jnp.bfloat16)
    return hi, (v - hi.astype(jnp.float32)).astype(jnp.bfloat16)


def nt_dot(a, b):
    return lax.dot_general(a, b, (((1,), (1,)), ((), ())), preferred_element_type=jnp.float32)


def kernel(
    nz, nc, kh, plants,
    f_ref, n_ref, mean_ref, spread_ref, cap_ref, kind_ref, plant_ref, out_ref,
    sitef, sitei, nown, nbuf, bsend, brecv, fown, frecv, fh, fl, par, onehot, acc, rsend, rrecv, zsend, zrecv,
    loc_sem, nx_send, nx_recv, fx_send, fx_recv, ring_send, ring_recv, r_send, r_recv, z_send, z_recv, plane_sem, twin_sem,
):
    half = nz // 2
    zero = half - 1
    near = half - 2
    peers = 2 * nc
    rows = 2 * nz
    row, col = lax.axis_index("row"), lax.axis_index("col")
    z, yh = row // 2, lax.rem(row, 2)
    partner = row + 1 - 2 * yh
    right = lax.rem(z + 1, nz) * 2 + yh
    left = lax.rem(z + nz - 1, nz) * 2 + yh
    mine = pl.multiple_of(yh * kh, kh)
    other = pl.multiple_of((1 - yh) * kh, kh)
    ua, up = 2 * yh, 2 - 2 * yh

    barrier = pltpu.get_barrier_semaphore()
    for r in (right, left):
        pl.semaphore_signal(barrier, inc=1, device_id=(r, col), device_id_type=MESH)

    core, yl, x = lax.rem(col, 2), lax.rem(col // 2, 2), col // 4
    nx = nc // 4
    group = [(row, lax.rem(x + i, nx) * 4 + yl * 2 + core) for i in range(1, nx)]
    flipped = col + 2 - 4 * yl
    group += [(partner, col), (row, flipped), (partner, flipped)]
    twin = (row, col + 1 - 2 * core)

    def signal(sem, who):
        pl.semaphore_signal(sem, inc=1, device_id=who, device_id_type=MESH)

    for who in group:
        signal(barrier, who)

    @pl.when(core == 0)
    def _():
        signal(barrier, twin)

    load_a = pltpu.make_async_copy(n_ref.at[pl.ds(0, 8), pl.ds(mine, kh)], nbuf.at[zero, ua], loc_sem.at[0])
    load_n = pltpu.make_async_copy(n_ref, nown, loc_sem.at[1])
    load_f = pltpu.make_async_copy(f_ref.at[:, pl.ds(mine, kh)], fown, loc_sem.at[2])
    floats, ints = (mean_ref, spread_ref, cap_ref), (kind_ref, plant_ref)
    load_s = [pltpu.make_async_copy(r, sitef.at[i], loc_sem.at[3 + i]) for i, r in enumerate(floats)]
    load_s += [pltpu.make_async_copy(r, sitei.at[i], loc_sem.at[6 + i]) for i, r in enumerate(ints)]
    load_n.start()
    load_a.start()
    for c in load_s:
        c.start()
    load_f.start()

    def to_partner(src, dst, i):
        return pltpu.make_async_remote_copy(
            src, dst, nx_send.at[i], nx_recv.at[i], device_id=(partner, col), device_id_type=MESH
        )

    q = kh // 2

    def ring(s, h, way):
        unit = (ua, ua, up, 1)[s]
        slot = zero - h if way == 0 else zero + h
        to = slot - 1 if way == 0 else slot + 1
        if s < 2:
            part = pl.ds(s * q, q)
        else:
            part = pl.ds(0, kh) if h < half - 1 else pl.ds(way * q, q)
        if h == half - 1:
            to = nz - 1
        src = nbuf.at[slot, unit, :, part]
        if s < 2 and h == 0:
            src = n_ref.at[pl.ds(0, 8), pl.ds(pl.multiple_of(mine + s * q, q), q)]
        i = (s * half + h) * 2 + way
        return pltpu.make_async_remote_copy(
            src, nbuf.at[to, unit, :, part], ring_send.at[i], ring_recv.at[i],
            device_id=(right if way == 0 else left, col), device_id_type=MESH,
        )

    def steps(s, h):
        return (s,) if s < 2 and h == half - 1 else (0, 1)

    pl.semaphore_wait(barrier, 2 + len(group) + core)
    for s in range(2):
        for way in range(2):
            ring(s, 0, way).start()

    swap_a = to_partner(n_ref.at[pl.ds(0, 8), pl.ds(other, kh)], nbuf.at[zero, ua], 0)
    swap_a.start()

    row_of = lax.broadcasted_iota(jnp.int32, (8, 128), 0)
    packed = jnp.zeros((8, 128), jnp.float32)
    for c in load_s:
        c.wait()
    for i in range(5):
        v = sitef[i : i + 1, :] if i < 3 else sitei[i - 3 : i - 2, :].astype(jnp.float32)
        packed = jnp.where(row_of == i, v, packed)
    par[yh] = packed
    load_n.wait()
    bsend[0:4, :] = nown[8:12, pl.ds(other, q)]
    bsend[4:8, :] = nown[8:12, pl.ds(pl.multiple_of(other + q, q), q)]
    swap_b = to_partner(bsend, brecv, 1)
    swap_p = to_partner(par.at[yh], par.at[yh], 2)
    swap_b.start()
    swap_p.start()
    swap_f = [
        pltpu.make_async_remote_copy(
            f_ref.at[pl.ds(i * 32, 32), pl.ds(other, kh)], frecv.at[pl.ds(i * 32, 32)],
            fx_send.at[i], fx_recv.at[i], device_id=(partner, col), device_id_type=MESH,
        )
        for i in range(4)
    ]
    for c in swap_f:
        c.start()

    sites = f_ref.shape[0]

    def split_f(src, base, i):
        @pl.loop(0, 4)
        def _(j):
            hi, lo = split_bf16(src[pl.ds(pl.multiple_of(i * 32, 32), 32), pl.ds(pl.multiple_of(j * (kh // 4), kh // 4), kh // 4)])
            at = pl.ds(pl.multiple_of(base + i * 32, 32), 32)
            cols = pl.ds(pl.multiple_of(j * (kh // 4), kh // 4), kh // 4)
            fh[at, cols] = hi
            fl[at, cols] = lo

    def build_t1():
        swap_b.wait_recv()
        for j in range(2):
            own = nown[8:12, pl.ds(pl.multiple_of(mine + j * q, q), q)]
            got = brecv[4 * j : 4 * j + 4, :]
            both = jnp.concatenate([own, got], axis=0)
            flip = jnp.concatenate([got, own], axis=0)
            nbuf[zero, 1, :, j * q : (j + 1) * q] = jnp.where(yh == 0, both, flip)

    def build_onehot():
        ids = jnp.concatenate([par[0], par[1]], axis=1)[4:5, :]
        ids = jnp.broadcast_to(ids, (128, 2 * sites))
        ids = ids.T

        @pl.loop(0, plants // 128)
        def _(j):
            lane = lax.broadcasted_iota(jnp.int32, (2 * sites, 128), 1) + j * 128
            onehot[:, pl.ds(pl.multiple_of(j * 128, 128), 128)] = jnp.where(ids == lane.astype(jnp.float32), 1.0, 0.0).astype(jnp.bfloat16)

    def matmul(slots, parts, k_from, k_to, units=()):
        step = kh // parts
        m = 24 * len(slots) + 8 * len(units)

        @pl.loop(k_from, k_to)
        def _(k):
            cols = pl.ds(pl.multiple_of(k * step, step), step)
            x = [nbuf[s, :, :, cols].reshape(24, step) for s in slots]
            x = jnp.concatenate(x + [nbuf[nz - 1, u, :, cols] for u in units], axis=0)
            hi = x.astype(jnp.bfloat16).astype(jnp.float32)
            hl = jnp.concatenate([hi, x - hi], axis=0).astype(jnp.bfloat16)
            t = nt_dot(hl, fh[:, cols])
            t = t[0:m] + t[m : 2 * m] + nt_dot(hl[0:m], fl[:, cols])

            @pl.when(k == 0)
            def _():
                acc[0:m, :] = t

            @pl.when(k != 0)
            def _():
                acc[0:m, :] += t

    def send_partials(slots, first=0):
        me = yh * nc + col
        for i, s in enumerate(slots, first):
            block = lax.rem(z + s - zero + nz, nz)
            t1 = acc[24 * i + 8 : 24 * i + 16, :]
            for y in range(2):
                a = acc[24 * i + 16 * y : 24 * i + 16 * y + 8, :]
                b = t1[4 * y : 4 * y + 4, :]
                b = jnp.concatenate([b[:, 0:128], b[:, 128:256]], axis=0)
                msg = jnp.concatenate([a, b], axis=1)
                self_ = jnp.logical_and(block == col, yh == y)

                @pl.when(self_)
                def _():
                    rrecv[me] = msg

                @pl.when(jnp.logical_not(self_))
                def _():
                    rsend[2 * s + y] = msg
                    pltpu.make_async_remote_copy(
                        rsend.at[2 * s + y], rrecv.at[me], r_send, r_recv,
                        device_id=(z * 2 + y, block), device_id_type=MESH,
                    ).start()

    def send_last(y, msg, lanes):
        me, block = yh * nc + col, lax.rem(z + half, nz)
        self_ = jnp.logical_and(block == col, yh == y)

        @pl.when(self_)
        def _():
            rrecv[me, :, lanes] = msg

        @pl.when(jnp.logical_not(self_))
        def _():
            i = 2 * (nz - 1) + y
            rsend[i, :, lanes] = msg
            pltpu.make_async_remote_copy(
                rsend.at[i, :, lanes], rrecv.at[me, :, lanes], r_send, r_recv,
                device_id=(z * 2 + y, block), device_id_type=MESH,
            ).start()

    def finish_sites():
        pltpu.make_async_copy(rrecv.at[pl.ds(0, peers - 1)], rrecv.at[pl.ds(0, peers - 1)], r_recv).wait()
        tot = rrecv[0]
        for i in range(1, peers):
            tot = tot + rrecv[i]
        b = jnp.concatenate([tot[0:4, 256:384], tot[4:8, 256:384]], axis=1)
        a = tot[:, 0:256]
        samples = jnp.concatenate([a, a[6:8], b, b[0:2]], axis=0)
        p = jnp.concatenate([par[0], par[1]], axis=1)
        speed = p[0:1] + p[1:2] * samples
        positive = jnp.maximum(speed, 0.0)
        wind = jnp.clip((positive * positive * positive - 27.0) / (1728.0 - 27.0), 0.0, 1.0)
        solar = jnp.clip(speed / 12.0, 0.0, 1.0)
        power = jnp.where(p[3:4] == 1.0, solar, wind) * p[2:3]
        p0, rest = power.astype(jnp.bfloat16), power
        rest = rest - p0.astype(jnp.float32)
        p1 = rest.astype(jnp.bfloat16)
        p2 = (rest - p1.astype(jnp.float32)).astype(jnp.bfloat16)
        pieces = jnp.concatenate([p0, p1, p2], axis=0)
        low = lax.broadcasted_iota(jnp.int32, (8, 128), 1) < 64

        sums = jnp.dot(pieces, onehot[...], preferred_element_type=jnp.float32)
        sums = sums[0:16] + sums[16:32] + sums[32:48]
        for j in range(nz):
            a, c = sums[0:8, 128 * j : 128 * (j + 1)], sums[8:16, 128 * j : 128 * (j + 1)]
            msgs = jnp.where(low, a, pltpu.roll(c, 64, 1)), jnp.where(low, pltpu.roll(a, 64, 1), c)
            for y in range(2):
                zsend[2 * j + y] = msgs[y][0:6]

        zrecv[row] = zsend[row]

        @pl.loop(0, rows - 1)
        def _(i):
            k = i // 2
            away = half + (k + 1) // 2 * (2 * lax.rem(k, 2) - 1)
            r = jnp.where(i < rows - 2, lax.rem(z + away, nz) * 2 + lax.rem(i, 2), partner)
            pltpu.make_async_remote_copy(
                zsend.at[r], zrecv.at[row], z_send, z_recv, device_id=(r, col), device_id_type=MESH
            ).start()

    slots_a = list(range(zero - near, zero + near + 1))
    slots_b = [0, nz - 2]

    def forward(s, h):
        if h == 0 and s == 2:
            swap_a.wait_recv()
        if h == 0 and s == 3:
            build_t1()
        for way in range(2):
            if h:
                ring(s, h - 1, way).wait_recv()
            if way in steps(s, h):
                ring(s, h, way).start()

    for who in group:
        signal(plane_sem, who)

    @pl.when(core == 1)
    def _():
        signal(plane_sem, twin)

    forward(0, 1)
    forward(1, 1)
    load_f.wait()
    load_a.wait()
    pl.semaphore_wait(plane_sem, len(group) + 1 - core)
    signal(twin_sem, twin)
    for h in range(near):
        forward(2, h)
        forward(3, h)
        forward(0, h + 2)
        forward(1, h + 2)
        if h < 2:
            for i in range(2):
                split_f(fown, yh * sites, 2 * h + i)
        if h == min(2, near - 1):
            swap_p.wait_recv()
            build_onehot()
        for i in range(4):
            if h == max(near - 4 + i, 0):
                swap_f[i].wait_recv()
                split_f(frecv, (1 - yh) * sites, i)
    forward(2, near)
    forward(3, near)
    pl.semaphore_wait(twin_sem, 1)
    matmul(slots_a, 2, 0, 2)
    send_partials(slots_a[: near // 2])
    forward(2, near + 1)
    send_partials(slots_a[near // 2 :], near // 2)
    forward(3, near + 1)
    for s in range(3):
        for way in steps(s, half - 1):
            ring(s, half - 1, way).wait_recv()
    matmul(slots_b, 1, 0, 1, (0, 2))
    for y in range(2):
        send_last(y, acc[48 + 8 * y : 56 + 8 * y, :], pl.ds(0, 256))
    send_partials(slots_b)
    for way in range(2):
        ring(3, half - 1, way).wait_recv()
        matmul([], 2, way, way + 1, (1,))
    for y in range(2):
        b = acc[4 * y : 4 * y + 4, :]
        send_last(y, jnp.concatenate([b[:, 0:128], b[:, 128:256]], axis=0), pl.ds(256, 128))
    finish_sites()

    swap_a.wait_send()
    swap_b.wait_send()
    swap_p.wait_send()
    for c in swap_f:
        c.wait_send()
    for s in range(4):
        for h in range(half):
            for way in steps(s, h):
                ring(s, h, way).wait_send()
    pltpu.make_async_copy(rsend.at[pl.ds(0, peers - 1)], rsend.at[pl.ds(0, peers - 1)], r_send).wait()
    pltpu.make_async_copy(zsend.at[pl.ds(0, rows - 1)], zsend.at[pl.ds(0, rows - 1)], z_send).wait()
    pltpu.make_async_copy(zrecv.at[pl.ds(0, rows - 1)], zrecv.at[pl.ds(0, rows - 1)], z_recv).wait()
    s0, s1 = zrecv[0], zrecv[1]
    for i in range(1, nz):
        s0 = s0 + zrecv[2 * i]
        s1 = s1 + zrecv[2 * i + 1]
    out_ref[...] = jnp.concatenate([s0[:, 0:64], s0[:, 64:128], s1[:, 0:64], s1[:, 64:128]], axis=0)


def body(factor_band, normals, site_mean, site_spread, site_capacity, site_kind, site_plant):
    rows, nc = lax.axis_size("row"), lax.axis_size("col")
    nz = rows // 2
    half = nz // 2
    sites, k = factor_band.shape
    kh = k // 2
    plants = 64 * rows
    f32, bf16 = jnp.float32, jnp.bfloat16
    vmem = pl.BlockSpec(memory_space=pltpu.VMEM)
    hbm = pl.BlockSpec(memory_space=pltpu.HBM)
    dma = pltpu.SemaphoreType.DMA
    return pl.pallas_call(
        functools.partial(kernel, nz, nc, kh, plants),
        out_shape=pltpu.VMEM((24, 64), f32),
        in_specs=[hbm] * 7,
        out_specs=vmem,
        scratch_shapes=[
            pltpu.VMEM((3, 128), f32),
            pltpu.VMEM((2, 128), jnp.int32),
            pltpu.VMEM((12, k), f32),
            pltpu.VMEM((nz, 3, 8, kh), f32),
            pltpu.VMEM((8, kh // 2), f32),
            pltpu.VMEM((8, kh // 2), f32),
            pltpu.VMEM((sites, kh), f32),
            pltpu.VMEM((sites, kh), f32),
            pltpu.VMEM((2 * sites, kh), bf16),
            pltpu.VMEM((2 * sites, kh), bf16),
            pltpu.VMEM((2, 8, 128), f32),
            pltpu.VMEM((2 * sites, plants), bf16),
            pltpu.VMEM((24 * (nz - 3), 2 * sites), f32),
            pltpu.VMEM((2 * nc, 8, 384), f32),
            pltpu.VMEM((2 * nc, 8, 384), f32),
            pltpu.VMEM((rows, 6, 128), f32),
            pltpu.VMEM((rows, 6, 128), f32),
            dma((8,)), dma((3,)), dma((3,)), dma((4,)), dma((4,)),
            dma((8 * half,)), dma((8 * half,)),
            dma, dma, dma, dma,
            pltpu.SemaphoreType.REGULAR, pltpu.SemaphoreType.REGULAR,
        ],
        compiler_params=pltpu.CompilerParams(
            collective_id=0, has_side_effects=True, vmem_limit_bytes=48 * 1024 * 1024
        ),
        cost_estimate=pl.CostEstimate(flops=3 * 2 * 24 * nz * 2 * sites * kh, bytes_accessed=4 * sites * k, transcendentals=0),
        name="band_to_plants",
    )(*(pltpu.with_memory_space_constraint(v, pltpu.HBM) for v in (factor_band, normals.T, site_mean, site_spread, site_capacity, site_kind, site_plant)))


def solution(mesh):
    in_specs = (P("row", "col"), P("col", "row"), P("row"), P("row"), P("row"), P("row"), P("row"))
    return jax.shard_map(body, mesh=mesh, in_specs=in_specs, out_specs=P("col", "row"), check_vma=False)
```
